32 devices in a mesh: dom: 2 (over x), space: 16 (over z, y, core).
Axes of the slice: x: 2, y: 2, z: 4, core: 2. Of those that a mesh axis runs over, the one named last changes fastest.
Arguments:
- inputs: bfloat16 [2, 32, 2048, 2048], P('dom', None, 'space'), parts along dimension 0, may hold values from -10.5 to 10.5
- target: bfloat16 [2, 32, 2048, 2048], P('dom', None, 'space'), parts along dimension 0, may hold values from -6 to 6
- spectral_weight: float32 [64, 32, 32, 128], P('space'), may hold values from -18 to 18
- local_weight: bfloat16 [32, 32], replicated, may hold values from -1 to 1
- bias_term: float32 [32], replicated, may hold values from -3 to 3
Outputs:
- grad_input: bfloat16 [2, 32, 2048, 2048], P('dom', None, 'space'), parts along dimension 0
- grad_spectral: float32 [64, 64, 32, 128], P('space', 'dom'), parts along dimension 1
- grad_local: float32 [64, 32], P('dom'), parts along dimension 0
- grad_bias: float32 [64], P('dom'), parts along dimension 0
The draws below stay inside these ranges and needn't reach their ends.
There are 2 independent parts, one for each index of `dom`. The reference program is written for one: setup_inputs(seed, part) draws one part's arguments, and reference() takes and returns one part's arrays. A program takes and returns all parts, laid end to end along the dimension named above; an argument that names none is the same for every part. Nothing has to cross between parts.
All inputs are finite; a program needn't handle non-finite values.
Results may differ from the reference program's by a relative error of at most 0.014.
Values may be sent and summed in bfloat16 or wider, within the bound.
No kernel may reach another device: no remote copies, remote signals or barrier semaphores. Data moves between devices by JAX's collectives and lax.ppermute only.
A program may use at most 192 MiB of HBM per device.

```python
import math
import jax
import jax.numpy as jnp
from jax import lax

C = 32
H = 2048
W = 2048
KX = 64
KY = 64
STEPS = 1


def draw_inputs(key, part):
    row_place = jnp.arange(H, dtype=jnp.float32) / (H - 1) - 0.5
    noise_field = jax.random.truncated_normal(key, -6.0, 6.0, (STEPS, C, H, W), jnp.float32)
    factor = jnp.power(3.0, row_place)
    return (noise_field * factor[None, None, :, None]).astype(jnp.bfloat16)


def levels(rng, extent, pieces, low, high):
    gain = 1.0
    for dim, parts in pieces:
        heights = jax.random.uniform(jax.random.fold_in(jax.random.fold_in(rng, 6), dim), (parts,), jnp.float32, low / len(pieces), high / len(pieces))
        gain = gain * jnp.repeat(jnp.exp(heights), extent[dim] // parts).reshape((-1,) + (1,) * (len(extent) - 1 - dim))
    return gain


def centred(key, dims, width, bound, cuts=(), held_as=jnp.bfloat16):
    entries = jax.random.normal(key, dims, jnp.float32) * width
    if len(cuts) > 0:
        entries = levels(key, dims, cuts, -0.22, 0.18) * entries
    return jnp.clip(entries, min=-bound, max=bound).astype(held_as)


def setup_inputs(seed: int = 0, part: int = 0) -> dict:
    seeds = jax.random.split(jax.random.key(seed), 6)
    part_splits = jax.random.split(jax.random.fold_in(seeds[5], part), 6)
    inputs = draw_inputs(jax.random.fold_in(jax.random.fold_in(seeds[5], part), 71), part)
    target = centred(part_splits[1], (STEPS, C, H, W), 1.0, 6.0, ((2, 16),))
    spectral_weight = centred(seeds[2], (KY, C, C, 2 * KX), 3.0, 18.0, ((0, 16),), jnp.float32)
    local_weight = centred(seeds[3], (C, C), C ** -0.5, 1.0)
    bias_term = centred(seeds[4], (C,), 1.0, 3.0, (), jnp.float32)
    return dict(inputs=inputs, target=target, spectral_weight=spectral_weight, local_weight=local_weight, bias_term=bias_term)


PRECISE = lax.Precision.HIGHEST

def row_table():
    mode_index = jnp.arange(KY, dtype=jnp.int32)[:, None]
    column = jnp.arange(W, dtype=jnp.int32)[None, :]
    angles = (mode_index * column % W).astype(jnp.float32) * (2.0 * math.pi / W)
    factor = 1.0 / math.sqrt(H * W)
    return jnp.stack([jnp.cos(angles) * factor, -jnp.sin(angles) * factor]).astype(jnp.bfloat16)

def column_table(row_index):
    column = jnp.arange(KX, dtype=jnp.int32)
    frequency = jnp.where(column < KX // 2, column, column + H - KX)
    angles = (row_index[:, None] * frequency[None, :] % H).astype(jnp.float32) * (2.0 * math.pi / H)
    return jnp.concatenate([jnp.cos(angles), jnp.sin(angles)], axis=1)

def mode_weights(start_mode, mode_count):
    mode_index = start_mode + jnp.arange(mode_count, dtype=jnp.int32)
    return jnp.where(mode_index == 0, 1.0, 2.0).astype(jnp.float32)

def row_analysis(field_data, basis):
    return jnp.einsum('schw,pkw->kpsch', field_data.astype(jnp.float32), basis.astype(jnp.float32))

def row_synth(spectra, basis):
    return jnp.einsum('kpsch,pkw->schw', spectra.astype(jnp.float32), basis.astype(jnp.float32))

def column_modes(slab_part, basis):
    product = jnp.einsum('kpsch,hj->kpscj', slab_part, basis, precision=PRECISE)
    half_count = basis.shape[1] // 2
    real_part = product[:, 0, :, :, :half_count] + product[:, 1, :, :, half_count:]
    imag_part = product[:, 1, :, :, :half_count] - product[:, 0, :, :, half_count:]
    return jnp.concatenate([real_part, imag_part], axis=-1)

def column_synth(mode_data, basis):
    half_count = basis.shape[1] // 2
    real_part, imag_part = (mode_data[..., :half_count], mode_data[..., half_count:])
    cosines, sine_part = (basis[:, :half_count], basis[:, half_count:])
    first_part = jnp.einsum('ysok,hk->ysoh', real_part, cosines, precision=PRECISE) - jnp.einsum('ysok,hk->ysoh', imag_part, sine_part, precision=PRECISE)
    second = jnp.einsum('ysok,hk->ysoh', real_part, sine_part, precision=PRECISE) + jnp.einsum('ysok,hk->ysoh', imag_part, cosines, precision=PRECISE)
    return jnp.stack([first_part, second], axis=1).astype(jnp.bfloat16)

def split_complex(mode_data):
    half_count = mode_data.shape[-1] // 2
    return (mode_data[..., :half_count], mode_data[..., half_count:])

def mix_modes(input_modes, weight):
    spec_real, spec_imag = split_complex(input_modes)
    weight_real, weight_imag = split_complex(weight)
    form = 'ysck,ycok->ysok'
    out_real = jnp.einsum(form, spec_real, weight_real, precision=PRECISE) - jnp.einsum(form, spec_imag, weight_imag, precision=PRECISE)
    out_imag = jnp.einsum(form, spec_real, weight_imag, precision=PRECISE) + jnp.einsum(form, spec_imag, weight_real, precision=PRECISE)
    return jnp.concatenate([out_real, out_imag], axis=-1)

def mix_back(delta_modes, weight):
    delta_real, delta_imag = split_complex(delta_modes)
    weight_real, weight_imag = split_complex(weight)
    form = 'ysok,ycok->ysck'
    out_real = jnp.einsum(form, delta_real, weight_real, precision=PRECISE) + jnp.einsum(form, delta_imag, weight_imag, precision=PRECISE)
    out_imag = jnp.einsum(form, delta_imag, weight_real, precision=PRECISE) - jnp.einsum(form, delta_real, weight_imag, precision=PRECISE)
    return jnp.concatenate([out_real, out_imag], axis=-1)

def mix_grad(input_modes, delta_modes):
    spec_real, spec_imag = split_complex(input_modes)
    delta_real, delta_imag = split_complex(delta_modes)
    form = 'ysck,ysok->ycok'
    grad_real = jnp.einsum(form, spec_real, delta_real, precision=PRECISE) + jnp.einsum(form, spec_imag, delta_imag, precision=PRECISE)
    grad_imag = jnp.einsum(form, spec_real, delta_imag, precision=PRECISE) - jnp.einsum(form, spec_imag, delta_real, precision=PRECISE)
    return jnp.concatenate([grad_real, grad_imag], axis=-1)

def gelu_parts(value):
    normal_cdf = 0.5 * (1.0 + jax.scipy.special.erf(value * (1.0 / math.sqrt(2.0))))
    density = jnp.exp(-0.5 * value * value) * (1.0 / math.sqrt(2.0 * math.pi))
    return (value * normal_cdf, normal_cdf + value * density)

def reference(inputs, target, spectral_weight, local_weight, bias_term):
    row_basis = row_table()
    column_basis = column_table(jnp.arange(H, dtype=jnp.int32))
    mode_gain = mode_weights(0, KY)[:, None, None, None]
    input_modes = column_modes(row_analysis(inputs, row_basis), column_basis)
    mixed_modes = mix_modes(input_modes, spectral_weight) * mode_gain
    local_term = jnp.einsum('co,schw->sohw', local_weight.astype(jnp.float32), inputs.astype(jnp.float32))
    preact = row_synth(column_synth(mixed_modes, column_basis), row_basis) + local_term + bias_term[None, :, None, None]
    activated, derivative = gelu_parts(preact)
    delta_pre = ((activated - target.astype(jnp.float32)) * derivative).astype(jnp.bfloat16)
    delta_modes = column_modes(row_analysis(delta_pre, row_basis), column_basis) * mode_gain
    grad_spectral = mix_grad(input_modes, delta_modes)
    back_modes = mix_back(delta_modes, spectral_weight)
    back_local = jnp.einsum('co,sohw->schw', local_weight.astype(jnp.float32), delta_pre.astype(jnp.float32))
    grad_input = (row_synth(column_synth(back_modes, column_basis), row_basis) + back_local).astype(jnp.bfloat16)
    cell_count = STEPS * H * W
    grad_local = jnp.einsum('schw,sohw->co', inputs.astype(jnp.float32), delta_pre.astype(jnp.float32)) / cell_count
    grad_bias = lax.optimization_barrier(jnp.sum(delta_pre.astype(jnp.float32), axis=(0, 2, 3))) / cell_count
    return (grad_input, grad_spectral, grad_local, grad_bias)
```

```python
import functools
import math

import jax
import jax.numpy as jnp
import ml_dtypes
import numpy as np
from jax import lax
from jax.experimental import pallas as pl
from jax.experimental.pallas import tpu as pltpu
from jax.sharding import PartitionSpec as P

KX = 64
KY = 64
LANES = 2 * KX
GROUP = 8
F32 = jnp.float32
BF16 = jnp.bfloat16

dot = functools.partial(jnp.dot, preferred_element_type=F32)


def dot_last(a, b):
    return lax.dot_general(a, b, (((1,), (1,)), ((), ())), preferred_element_type=F32)


def params(mib=48):
    return pltpu.CompilerParams(vmem_limit_bytes=mib * 2**20)


def row_basis_table(height, width):
    angles = 2.0 * np.pi / width * (np.arange(KY)[:, None] * np.arange(width)[None, :] % width)
    factor = 1.0 / math.sqrt(height * width)
    table = np.concatenate([np.cos(angles) * factor, -np.sin(angles) * factor])
    return table.astype(np.float32).astype(ml_dtypes.bfloat16)


def column_tables(height):
    index = np.arange(KX)
    frequency = np.where(index < KX // 2, index, index + height - KX)
    angles = 2.0 * np.pi / height * (np.arange(height)[:, None] * frequency[None, :] % height)
    cosines, sines = np.cos(angles), np.sin(angles)

    def parts(table):
        high = table.astype(np.float32).astype(ml_dtypes.bfloat16)
        low = (table - high.astype(np.float64)).astype(np.float32).astype(ml_dtypes.bfloat16)
        return high, low

    synthesis = parts(np.concatenate([cosines, sines], axis=1))
    analysis = parts(np.concatenate([cosines, -sines, sines, cosines], axis=1))
    return np.concatenate(synthesis + analysis, axis=1)


def swap_halves(value):
    return pltpu.roll(value, LANES // 2, 1)


def real_lanes(shape):
    return lax.broadcasted_iota(jnp.int32, shape, 1) < LANES // 2


def column_analysis(row_modes, tables_ref):
    rows = row_modes[0].shape[0]
    first, second = LANES * 2, LANES * 3
    high = [tables_ref[:, first : first + LANES], tables_ref[:, second : second + LANES]]
    low = [tables_ref[:, first + 2 * LANES : first + 3 * LANES], tables_ref[:, second + 2 * LANES : second + 3 * LANES]]
    flipped = [value.T for value in row_modes]
    parts = [[value[:KY] for value in flipped], [value[KY:] for value in flipped]]
    parts = [jnp.concatenate(part, axis=0) for part in parts]
    if rows % 128 == 0:
        parts = [jnp.concatenate(parts, axis=1)]
        high = [jnp.concatenate(high, axis=0)]
        low = [jnp.concatenate(low, axis=0)]
    total = 0.0
    for part, table_high, table_low in zip(parts, high, low):
        part_high = part.astype(BF16)
        part_low = (part - part_high.astype(F32)).astype(BF16)
        total += dot(part_high, table_high) + dot(part_low, table_high) + dot(part_high, table_low)
    return [total[i * KY : (i + 1) * KY] for i in range(len(row_modes))]


def column_synthesis(modes_ref, channel, channels, tables_ref):
    modes = modes_ref[pl.ds(channel, KY, stride=channels), :]
    real = real_lanes(modes.shape)
    both = jnp.concatenate([jnp.where(real, modes, -modes), swap_halves(modes)], axis=0).astype(BF16)
    both = jnp.concatenate([both, both], axis=1)
    return dot_last(tables_ref[:, : 2 * LANES], both).astype(BF16)


def gelu_parts(value):
    normal_cdf = 0.5 * (1.0 + lax.erf(value * (1.0 / math.sqrt(2.0))))
    density = jnp.exp(-0.5 * value * value) * (1.0 / math.sqrt(2.0 * math.pi))
    return (value * normal_cdf, normal_cdf + value * density)


def emit_halves(modes, send_ref, keep_ref):
    half = modes.shape[0] // 2
    keep_ref[...] = modes[:half]
    send_ref[...] = modes[half:].astype(BF16)


def analysis_kernel(block, channels, field_ref, basis_ref, tables_ref, send_ref, keep_ref, modes):
    step = pl.program_id(0)
    rows, width = field_ref.shape[1:]
    product = dot(field_ref[...].reshape(block * rows, width), basis_ref[...])
    parts = column_analysis([product[i * rows : (i + 1) * rows] for i in range(block)], tables_ref)
    for i, part in enumerate(parts):
        modes[pl.ds(step * block + i, KY, stride=channels), :] = part

    @pl.when(step == pl.num_programs(0) - 1)
    def _():
        emit_halves(modes, send_ref, keep_ref)


def half_outputs(channels):
    half = KY // 2 * channels
    specs = [pl.BlockSpec((half, LANES), lambda *_: (0, 0))] * 2
    shapes = [jax.ShapeDtypeStruct((half, LANES), BF16), jax.ShapeDtypeStruct((half, LANES), F32)]
    return specs, shapes


def analyse(field, basis_t, tables, block=4):
    channels, rows, width = field.shape
    specs, shapes = half_outputs(channels)
    return pl.pallas_call(
        functools.partial(analysis_kernel, block, channels),
        grid=(channels // block,),
        in_specs=[
            pl.BlockSpec((block, rows, width), lambda i: (i, 0, 0)),
            pl.BlockSpec(basis_t.shape, lambda i: (0, 0)),
            pl.BlockSpec(tables.shape, lambda i: (0, 0)),
        ],
        out_specs=specs,
        out_shape=shapes,
        scratch_shapes=[pltpu.VMEM((KY * channels, LANES), F32)],
        compiler_params=params(),
        name="analyse",
    )(field, basis_t, tables)


def group_rows(value, start):
    channels, _, width = value.shape
    return value[:, start : start + GROUP, :].reshape(channels * GROUP, width).astype(BF16)


def local_kernel(chunk, field_ref, weight_ref, bias_ref, _, out_ref):
    channels, rows, width = field_ref.shape
    for start in range(0, width, chunk):
        columns = pl.ds(start, chunk)
        field = field_ref[:, :, columns].astype(F32)
        parts = []
        for row in range(0, rows, GROUP):
            part = dot(weight_ref[...], group_rows(field, row)) + bias_ref[...]
            parts.append(part.reshape(channels, GROUP, chunk))
        out_ref[:, :, columns] = jnp.concatenate(parts, axis=1).astype(BF16)


def mix_local(field, weight, bias, out, first, count, block=16, chunk=512):
    channels, rows, width = field.shape
    offset = first // block
    spec = pl.BlockSpec((channels, block, width), lambda i: (0, offset + i, 0))
    whole = lambda array: pl.BlockSpec(array.shape, lambda i: (0, 0))
    return pl.pallas_call(
        functools.partial(local_kernel, chunk),
        grid=(count // block,),
        in_specs=[spec, whole(weight), whole(bias), pl.BlockSpec(memory_space=pl.ANY)],
        out_specs=spec,
        out_shape=jax.ShapeDtypeStruct(field.shape, BF16),
        input_output_aliases={3: 0},
        compiler_params=params(),
        name="mix_local",
    )(field, weight, bias, out)


def back_kernel(chunk, field_ref, delta_ref, weight_ref, _, out_ref, grad_ref):
    channels, rows, width = field_ref.shape
    grad = jnp.zeros(grad_ref.shape, F32)
    for start in range(0, width, chunk):
        columns = pl.ds(start, chunk)
        field = field_ref[:, :, columns].astype(F32)
        delta = delta_ref[:, :, columns].astype(F32)
        parts = []
        for row in range(0, rows, GROUP):
            delta_group = group_rows(delta, row)
            grad += dot_last(group_rows(field, row), delta_group)
            parts.append(dot(weight_ref[...], delta_group).reshape(channels, GROUP, chunk))
        out_ref[:, :, columns] = jnp.concatenate(parts, axis=1).astype(BF16)

    @pl.when(pl.program_id(0) == 0)
    def _():
        grad_ref[...] = grad

    @pl.when(pl.program_id(0) > 0)
    def _():
        grad_ref[...] += grad


def mix_back_local(field, delta, weight, out, first, count, block=16, chunk=512):
    channels, rows, width = field.shape
    offset = first // block
    spec = pl.BlockSpec((channels, block, width), lambda i: (0, offset + i, 0))
    whole = pl.BlockSpec(weight.shape, lambda i: (0, 0))
    return pl.pallas_call(
        functools.partial(back_kernel, chunk),
        grid=(count // block,),
        in_specs=[spec, spec, whole, pl.BlockSpec(memory_space=pl.ANY)],
        out_specs=[spec, whole],
        out_shape=[jax.ShapeDtypeStruct(field.shape, BF16), jax.ShapeDtypeStruct(weight.shape, F32)],
        input_output_aliases={3: 0},
        compiler_params=params(),
        name="mix_back_local",
    )(field, delta, weight, out)


def load_modes(modes, first_ref, second_ref):
    half = first_ref.shape[0]
    modes[:half] = first_ref[...].astype(F32)
    modes[half:] = second_ref[...].astype(F32)


def delta_kernel(
    block, channels, chunk, local_ref, target_ref, first_ref, second_ref, basis_ref, basis_t_ref, tables_ref,
    delta_ref, send_ref, keep_ref, sums_ref, mixed, modes,
):
    step = pl.program_id(0)
    rows, width = local_ref.shape[1:]

    @pl.when(step == 0)
    def _():
        load_modes(mixed, first_ref, second_ref)

    spectra = jnp.concatenate(
        [column_synthesis(mixed, step * block + i, channels, tables_ref) for i in range(block)], axis=0
    )
    product = jnp.zeros((block * rows, LANES), F32)
    for start in range(0, width, chunk):
        columns = pl.ds(start, chunk)
        local = local_ref[:, :, columns].reshape(block * rows, chunk).astype(F32)
        target = target_ref[:, :, columns].reshape(block * rows, chunk).astype(F32)
        activated, derivative = gelu_parts(dot(spectra, basis_ref[:, columns]) + local)
        delta = ((activated - target) * derivative).astype(BF16)
        delta_ref[:, :, columns] = delta.reshape(block, rows, chunk)
        product += dot(delta, basis_t_ref[columns, :])
    row_modes = [product[i * rows : (i + 1) * rows] for i in range(block)]
    for i, part in enumerate(column_analysis(row_modes, tables_ref)):
        modes[pl.ds(step * block + i, KY, stride=channels), :] = part
        sums_ref[pl.ds(step * block + i, 1), :] = jnp.sum(row_modes[i], axis=0, keepdims=True)

    @pl.when(step == pl.num_programs(0) - 1)
    def _():
        emit_halves(modes, send_ref, keep_ref)


def make_delta(local, target, first, second, basis, basis_t, tables, block=4, chunk=512):
    channels, rows, width = local.shape
    field = pl.BlockSpec((block, rows, width), lambda i: (i, 0, 0))
    whole = lambda array: pl.BlockSpec(array.shape, lambda i: (0, 0))
    specs, shapes = half_outputs(channels)
    scratch = pltpu.VMEM((KY * channels, LANES), F32)
    return pl.pallas_call(
        functools.partial(delta_kernel, block, channels, chunk),
        grid=(channels // block,),
        in_specs=[field, field] + [whole(array) for array in (first, second, basis, basis_t, tables)],
        out_specs=[field] + specs + [pl.BlockSpec((channels, LANES), lambda i: (0, 0))],
        out_shape=[jax.ShapeDtypeStruct(local.shape, BF16)]
        + shapes
        + [jax.ShapeDtypeStruct((channels, LANES), F32)],
        scratch_shapes=[scratch, scratch],
        compiler_params=params(),
        name="make_delta",
    )(local, target, first, second, basis, basis_t, tables)


def synthesis_kernel(
    block, channels, chunk, offset, local_ref, first_ref, second_ref, basis_ref, tables_ref, _, out_ref, modes
):
    step = pl.program_id(0)
    rows, width = local_ref.shape[1:]

    @pl.when(step == 0)
    def _():
        load_modes(modes, first_ref, second_ref)

    spectra = jnp.concatenate(
        [column_synthesis(modes, (offset + step) * block + i, channels, tables_ref) for i in range(block)], axis=0
    )
    for start in range(0, width, chunk):
        columns = pl.ds(start, chunk)
        local = local_ref[:, :, columns].reshape(block * rows, chunk).astype(F32)
        value = dot(spectra, basis_ref[:, columns]) + local
        out_ref[:, :, columns] = value.astype(BF16).reshape(block, rows, chunk)


def synthesise(local, first, second, basis, tables, out, start, count, block=4, chunk=512):
    channels, rows, width = local.shape
    offset = start // block
    field = pl.BlockSpec((block, rows, width), lambda i: (offset + i, 0, 0))
    whole = lambda array: pl.BlockSpec(array.shape, lambda i: (0, 0))
    return pl.pallas_call(
        functools.partial(synthesis_kernel, block, channels, chunk, offset),
        grid=(count // block,),
        in_specs=[field]
        + [whole(array) for array in (first, second, basis, tables)]
        + [pl.BlockSpec(memory_space=pl.ANY)],
        out_specs=field,
        out_shape=jax.ShapeDtypeStruct(local.shape, BF16),
        scratch_shapes=[pltpu.VMEM((KY * channels, LANES), F32)],
        input_output_aliases={5: 0},
        compiler_params=params(),
        name="synthesise",
    )(local, first, second, basis, tables, out)


def sum_parts(refs):
    return functools.reduce(lambda a, b: a + b, [ref[...].astype(F32) for ref in refs])


def mix_modes_kernel(count, channels, *refs):
    parts, (weight_ref, gain_ref, mixed_ref, modes_ref) = refs[:-4], refs[-4:]
    modes_ref[...] = sum_parts(parts)
    real = real_lanes((channels, LANES))
    for q in range(count):
        rows = slice(q * channels, (q + 1) * channels)
        modes = modes_ref[rows]
        other = swap_halves(modes)
        first, second = jnp.where(real, modes, other), jnp.where(real, other, -modes)
        direct = jnp.zeros((channels, LANES), F32)
        crossed = jnp.zeros((channels, LANES), F32)
        for c in range(channels):
            weight = weight_ref[q, c]
            direct += first[c : c + 1] * weight
            crossed += second[c : c + 1] * weight
        mixed_ref[rows] = ((direct + swap_halves(crossed)) * gain_ref[q : q + 1]).astype(BF16)


def mix_modes(parts, weight, gain):
    count, channels = weight.shape[:2]
    return pl.pallas_call(
        functools.partial(mix_modes_kernel, count, channels),
        out_shape=[
            jax.ShapeDtypeStruct((count * channels, LANES), BF16),
            jax.ShapeDtypeStruct((count * channels, LANES), F32),
        ],
        compiler_params=params(),
        name="mix_modes",
    )(*parts, weight, gain)


def mix_back_kernel(count, channels, *refs):
    parts, (weight_ref, gain_ref, back_ref, delta_ref) = refs[:-4], refs[-4:]
    delta_ref[...] = sum_parts(parts)
    real = real_lanes((channels, LANES))
    for q in range(count):
        rows = slice(q * channels, (q + 1) * channels)
        delta = delta_ref[rows] * gain_ref[q : q + 1]
        delta_ref[rows] = delta
        other = swap_halves(delta)
        first, second = jnp.where(real, delta, -other), jnp.where(real, other, delta)
        direct, crossed = [], []
        for c in range(channels):
            weight = weight_ref[q, c]
            direct.append(jnp.sum(first * weight, axis=0, keepdims=True))
            crossed.append(jnp.sum(second * weight, axis=0, keepdims=True))
        direct, crossed = jnp.concatenate(direct, axis=0), jnp.concatenate(crossed, axis=0)
        back_ref[rows] = (direct + swap_halves(crossed)).astype(BF16)


def mix_back(parts, weight, gain):
    count, channels = weight.shape[:2]
    return pl.pallas_call(
        functools.partial(mix_back_kernel, count, channels),
        out_shape=[
            jax.ShapeDtypeStruct((count * channels, LANES), BF16),
            jax.ShapeDtypeStruct((count * channels, LANES), F32),
        ],
        compiler_params=params(),
        name="mix_back",
    )(*parts, weight, gain)


def grad_kernel(channels, modes_ref, delta_ref, grad_ref):
    modes, delta = modes_ref[...], delta_ref[...]
    real = real_lanes(modes.shape)
    other, delta_other = swap_halves(modes), swap_halves(delta)
    first, second = jnp.where(real, modes, other), jnp.where(real, other, -modes)
    for c in range(channels):
        grad_ref[0, c] = first[c : c + 1] * delta + second[c : c + 1] * delta_other


def mode_grad(modes, delta, count, channels):
    spec = pl.BlockSpec((channels, LANES), lambda i: (i, 0))
    return pl.pallas_call(
        functools.partial(grad_kernel, channels),
        grid=(count,),
        in_specs=[spec, spec],
        out_specs=pl.BlockSpec((1, channels, channels, LANES), lambda i: (i, 0, 0, 0)),
        out_shape=jax.ShapeDtypeStruct((count, channels, channels, LANES), F32),
        name="mode_grad",
    )(modes, delta)


def fold_kernel(channels, *refs):
    parts, out_ref = refs[:-1], refs[-1]
    size = channels * GROUP
    total = sum_parts(parts)
    row = lax.broadcasted_iota(jnp.int32, (size, size), 0) % GROUP
    column = lax.broadcasted_iota(jnp.int32, (size, size), 1) % GROUP
    total = jnp.where(row == column, total, 0.0)
    wide = lax.broadcasted_iota(jnp.int32, (channels, size), 1) // GROUP
    pick = (wide == lax.broadcasted_iota(jnp.int32, (channels, size), 0)).astype(F32)
    half = jnp.dot(pick, total, precision=lax.Precision.HIGHEST, preferred_element_type=F32)
    out_ref[...] = lax.dot_general(
        half, pick, (((1,), (1,)), ((), ())), precision=lax.Precision.HIGHEST, preferred_element_type=F32
    )


def fold_groups(parts, channels):
    return pl.pallas_call(
        functools.partial(fold_kernel, channels),
        out_shape=jax.ShapeDtypeStruct((channels, channels), F32),
        name="fold_groups",
    )(*parts)


def blank(shape):
    def kernel(out_ref):
        pass

    return pl.pallas_call(
        kernel,
        out_specs=pl.BlockSpec(memory_space=pl.ANY),
        out_shape=jax.ShapeDtypeStruct(shape, BF16),
        name="blank",
    )()


def per_device(devices, inputs, target, spectral_weight, local_weight, bias_term):
    samples, channels, rows, width = inputs.shape
    assert samples == 1
    field, target = inputs[0], target[0]
    height = rows * devices
    count = spectral_weight.shape[0]
    device = lax.axis_index("space")
    far = devices // 4

    place = np.arange(KY) // count
    offset = place // (2 * far) + 2 * (place // far % 2) + 4 * (place % far)
    order = (device ^ jnp.asarray(offset, jnp.int32)) * count + jnp.asarray(np.arange(KY) % count, jnp.int32)
    source = jnp.concatenate([order, order + KY])
    pick = (jnp.arange(LANES, dtype=jnp.int32)[:, None] == source[None, :]).astype(BF16)
    basis_table = row_basis_table(height, width)
    basis_t = dot(jnp.asarray(basis_table.T.copy()), pick).astype(BF16)
    tables = lax.dynamic_slice_in_dim(jnp.asarray(column_tables(height)), device * rows, rows, 0)
    mode_index = device * count + jnp.arange(count, dtype=jnp.int32)
    gain = jnp.broadcast_to(jnp.where(mode_index == 0, 1.0, 2.0).astype(F32)[:, None], (count, LANES))

    def exchange(value, mask):
        return lax.ppermute(value, "space", [(i, i ^ mask) for i in range(devices)])

    barrier = lax.optimization_barrier

    def beside(sent, received, work, state):
        if work is None:
            return received, state
        sent, state = barrier((sent, state))
        return barrier((received, work(state)))

    def reduce_modes(send, keep, work, state):
        received = exchange(send, 1).astype(F32)
        half = keep.shape[0] // 2
        send = (keep[half:] + received[half:]).astype(BF16)
        keep = keep[:half] + received[:half]
        received, state = beside(send, exchange(send, 2), work[0], state)
        total = keep + received.astype(F32)
        size = total.shape[0] // far
        pieces = [total[i * size : (i + 1) * size].astype(BF16) for i in range(1, far)]
        received, state = beside(pieces, [exchange(p, 4 * (i + 1)) for i, p in enumerate(pieces)], work[1], state)
        return [total[:size]] + received, state

    def gather_modes(own, work, state):
        received, state = beside(own, [exchange(own, 4 * i) for i in range(1, far)], work[0], state)
        part = jnp.concatenate([own] + received, axis=0)
        received, state = beside(part, exchange(part, 2), work[1], state)
        part = jnp.concatenate([part, received], axis=0)
        return part, exchange(part, 1), state

    send, keep = analyse(field, basis_t, tables)
    kron = lambda matrix: jnp.kron(matrix, jnp.eye(GROUP, dtype=BF16))
    forward_weight, back_weight = kron(local_weight.T), kron(local_weight)
    bias = jnp.repeat(bias_term, GROUP)[:, None]
    splits = 4 if rows % 64 == 0 else 1
    step = rows // splits

    def local_work(i):
        if i >= splits:
            return None
        return lambda state: mix_local(field, forward_weight, bias, state, i * step, step)

    local = blank(field.shape)
    parts, local = reduce_modes(send, keep, [local_work(0), local_work(1)], local)
    mixed, modes = mix_modes(parts, spectral_weight, gain)
    first, second, local = gather_modes(mixed, [local_work(2), local_work(3)], local)
    basis = lax.dot_general(pick, jnp.asarray(basis_table), (((0,), (0,)), ((), ())), preferred_element_type=F32)
    basis = basis.astype(BF16)
    delta, send, keep, sums = make_delta(local, target, first, second, basis, basis_t, tables)

    def back_work(i):
        if i >= splits:
            return None

        def work(state):
            out, grads = state
            out, grad = mix_back_local(field, delta, back_weight, out, i * step, step)
            return out, grads + [grad]

        return work

    parts, state = reduce_modes(send, keep, [back_work(0), back_work(1)], (local, []))
    back, delta_modes = mix_back(parts, spectral_weight, gain)
    first, second, state = gather_modes(back, [back_work(2), back_work(3)], state)
    back_local, grads = state
    grad_spectral = mode_grad(modes, delta_modes, count, channels)

    def tree(values):
        while len(values) > 1:
            values = [values[i] + values[i + 1] for i in range(0, len(values), 2)]
        return values[0]

    bias_sum = jnp.sum(jnp.where(source[None, :] == 0, sums, 0.0), axis=1) * math.sqrt(height * width)
    shared = jnp.concatenate([fold_groups(grads, channels), bias_sum[:, None]], axis=1)
    split = channels // 2
    near = [exchange(shared, i) for i in range(1, 4)]
    near, grad_input = beside(
        shared, near, lambda out: synthesise(back_local, first, second, basis, tables, out, 0, split), delta
    )
    shared = tree([shared] + near)
    distant = [exchange(shared, 4 * i) for i in range(1, far)]
    distant, grad_input = beside(
        shared, distant, lambda out: synthesise(back_local, first, second, basis, tables, out, split, channels - split),
        grad_input,
    )
    shared = tree([shared] + distant) / (samples * height * width)
    return (grad_input[None], grad_spectral, shared[:, :channels], shared[:, channels])


def solution(mesh):
    return jax.shard_map(
        functools.partial(per_device, mesh.shape["space"]),
        mesh=mesh,
        in_specs=(
            P("dom", None, "space", None),
            P("dom", None, "space", None),
            P("space", None, None, None),
            P(),
            P(),
        ),
        out_specs=(
            P("dom", None, "space", None),
            P("space", "dom", None, None),
            P("dom", None),
            P("dom"),
        ),
        check_vma=False,
    )
```

```python
import functools
import math

import jax
import jax.numpy as jnp
import ml_dtypes
import numpy as np
from jax import lax
from jax.experimental import pallas as pl
from jax.experimental.pallas import tpu as pltpu
from jax.sharding import PartitionSpec as P

KX = 64
KY = 64
LANES = 2 * KX
GROUP = 8
F32 = jnp.float32
BF16 = jnp.bfloat16
SCALE = math.sqrt(0.5)

dot = functools.partial(jnp.dot, preferred_element_type=F32)


def dot_last(a, b):
    return lax.dot_general(a, b, (((1,), (1,)), ((), ())), preferred_element_type=F32)


def params(mib):
    return pltpu.CompilerParams(vmem_limit_bytes=mib * 2**20)


def row_basis_table(height, width):
    angles = 2.0 * np.pi / width * (np.arange(KY)[:, None] * np.arange(width)[None, :] % width)
    factor = 1.0 / math.sqrt(height * width)
    table = np.concatenate([np.cos(angles) * factor, -np.sin(angles) * factor])
    return table.astype(np.float32).astype(ml_dtypes.bfloat16)


def column_tables(height):
    index = np.arange(KX)
    frequency = np.where(index < KX // 2, index, index + height - KX)
    angles = 2.0 * np.pi / height * (np.arange(height)[:, None] * frequency[None, :] % height)
    cosines, sines = np.cos(angles), np.sin(angles)

    def parts(table):
        high = table.astype(np.float32).astype(ml_dtypes.bfloat16)
        low = (table - high.astype(np.float64)).astype(np.float32).astype(ml_dtypes.bfloat16)
        return high, low

    synthesis = parts(np.concatenate([cosines, sines], axis=1))
    analysis = parts(np.concatenate([cosines, -sines, sines, cosines], axis=1))
    return np.concatenate(synthesis + analysis, axis=1)


def swap_halves(value):
    return pltpu.roll(value, LANES // 2, 1)


def real_lanes(shape):
    return lax.broadcasted_iota(jnp.int32, shape, 1) < LANES // 2


def column_analysis(row_modes, tables_ref):
    rows = row_modes[0].shape[0]
    first, second = LANES * 2, LANES * 3
    high = [tables_ref[:, first : first + LANES], tables_ref[:, second : second + LANES]]
    low = [tables_ref[:, first + 2 * LANES : first + 3 * LANES], tables_ref[:, second + 2 * LANES : second + 3 * LANES]]
    flipped = [value.T for value in row_modes]
    parts = [[value[:KY] for value in flipped], [value[KY:] for value in flipped]]
    parts = [jnp.concatenate(part, axis=0) for part in parts]
    if rows % 128 == 0:
        parts = [jnp.concatenate(parts, axis=1)]
        high = [jnp.concatenate(high, axis=0)]
        low = [jnp.concatenate(low, axis=0)]
    total = 0.0
    for part, table_high, table_low in zip(parts, high, low):
        part_high = part.astype(BF16)
        part_low = (part - part_high.astype(F32)).astype(BF16)
        total += dot(part_high, table_high) + dot(part_low, table_high) + dot(part_high, table_low)
    return [total[i * KY : (i + 1) * KY] for i in range(len(row_modes))]


def column_synthesis(modes_ref, channel, channels, tables_ref):
    modes = modes_ref[pl.ds(channel, KY, stride=channels), :]
    real = real_lanes(modes.shape)
    both = jnp.concatenate([jnp.where(real, modes, -modes), swap_halves(modes)], axis=0).astype(BF16)
    both = jnp.concatenate([both, both], axis=1)
    return dot_last(tables_ref[:, : 2 * LANES], both).astype(BF16)


def twice_delta(value, target):
    cdf = 1.0 + lax.erf(value)
    density = jnp.exp2(value * (value * -math.log2(math.e))) * (2.0 / math.sqrt(math.pi))
    value, cdf, density = value.astype(BF16), cdf.astype(BF16), density.astype(BF16)
    return (value * cdf * BF16(SCALE) - target) * (cdf + value * density)


def store_modes(product, first, block, tables_ref, modes):
    rows = product.shape[0] // block
    channels = modes.shape[0] // KY
    parts = column_analysis([product[i * rows : (i + 1) * rows] for i in range(block)], tables_ref)
    for i, part in enumerate(parts):
        modes[pl.ds(first + i, KY, stride=channels), :] = part


def emit_halves(modes, send_ref, keep_ref):
    half = modes.shape[0] // 2
    keep_ref[...] = modes[:half]
    send_ref[...] = modes[half:].astype(BF16)


VMEM = pl.BlockSpec(memory_space=pltpu.VMEM)
HBM = pl.BlockSpec(memory_space=pl.ANY)


def in_vmem(array):
    return pltpu.with_memory_space_constraint(array, pltpu.VMEM)


def in_hbm(array):
    return pltpu.with_memory_space_constraint(array, pltpu.HBM)


def half_shapes(channels):
    half = KY // 2 * channels
    return [jax.ShapeDtypeStruct((half, LANES), BF16), jax.ShapeDtypeStruct((half, LANES), F32)]


def analysis_kernel(block, field_ref, basis_ref, tables_ref, send_ref, keep_ref, held_ref, modes, sems):
    channels, rows, width = field_ref.shape
    copies = [pltpu.make_async_copy(field_ref.at[i], held_ref.at[i], sems.at[i]) for i in range(channels)]
    for copy in copies:
        copy.start()
    product = None
    for start in range(0, channels + block, block):
        before, product = product, None
        if start < channels:
            for copy in copies[start : start + block]:
                copy.wait()
            product = dot(held_ref[pl.ds(start, block)].reshape(block * rows, width), basis_ref[...])
        if before is not None:
            store_modes(before, start - block, block, tables_ref, modes)
    emit_halves(modes, send_ref, keep_ref)


def analyse(field, basis_t, tables, block=2):
    channels = field.shape[0]
    return pl.pallas_call(
        functools.partial(analysis_kernel, block),
        in_specs=[HBM, VMEM, VMEM],
        out_specs=[VMEM] * 2,
        out_shape=half_shapes(channels),
        scratch_shapes=[pltpu.VMEM(field.shape, BF16), pltpu.VMEM((KY * channels, LANES), F32), pltpu.SemaphoreType.DMA((channels,))],
        compiler_params=params(24),
        name="analyse",
    )(in_hbm(field), basis_t, tables)


def group_rows(value, start):
    channels, _, width = value.shape
    return value[:, start : start + GROUP, :].reshape(channels * GROUP, width).astype(BF16)


def picks(channels):
    size = channels * GROUP
    wide = lax.broadcasted_iota(jnp.int32, (channels, size), 1) // GROUP
    return (wide == lax.broadcasted_iota(jnp.int32, (channels, size), 0)).astype(BF16)


def same_row(size):
    row = lax.broadcasted_iota(jnp.int32, (size, size), 0) % GROUP
    return row == lax.broadcasted_iota(jnp.int32, (size, size), 1) % GROUP


def spread_weight(weight):
    pick = picks(weight.shape[0])
    wide = dot(weight, pick).astype(BF16)
    full = lax.dot_general(pick, wide, (((0,), (0,)), ((), ())), preferred_element_type=F32)
    return jnp.where(same_row(pick.shape[1]), full, 0.0).astype(BF16)


def fetch_rows(field_ref, held, sems, first, block):
    copies = [
        pltpu.make_async_copy(field_ref.at[:, pl.ds(first + i * block, block)], held.at[i], sems.at[i])
        for i in range(held.shape[0])
    ]
    for copy in copies:
        copy.start()
    return copies


def local_kernel(first, chunk, field_ref, weight_ref, bias_ref, *rest):
    out_ref, held, sems = rest[-3:]
    blocks, channels, block, width = held.shape
    copies = fetch_rows(field_ref, held, sems, first, block)
    weight = spread_weight(weight_ref[...])
    bias = lax.dot_general(
        picks(channels).astype(F32), bias_ref[...], (((0,), (0,)), ((), ())),
        precision=lax.Precision.HIGHEST, preferred_element_type=F32,
    )
    for i, copy in enumerate(copies):
        copy.wait()
        rows = slice(first + i * block, first + (i + 1) * block)
        for start in range(0, width, chunk):
            columns = pl.ds(start, chunk)
            field = held[i, :, :, columns].astype(F32)
            parts = []
            for group in range(0, block, GROUP):
                part = (dot(weight, group_rows(field, group)) + bias) * SCALE
                parts.append(part.reshape(channels, GROUP, chunk))
            out_ref[:, rows, columns] = jnp.concatenate(parts, axis=1).astype(BF16)


def row_scratch(field, count, block):
    channels, _, width = field.shape
    blocks = count // block
    return [pltpu.VMEM((blocks, channels, block, width), BF16), pltpu.SemaphoreType.DMA((blocks,))]


def mix_local(field, weight, bias, out, first, count, block=16, chunk=512):
    more = [] if out is None else [in_vmem(out)]
    return pl.pallas_call(
        functools.partial(local_kernel, first, chunk),
        in_specs=[HBM] + [VMEM] * (2 + len(more)),
        out_specs=VMEM,
        out_shape=pltpu.VMEM(field.shape, BF16),
        scratch_shapes=row_scratch(field, count, block),
        input_output_aliases={3: 0} if more else {},
        compiler_params=params(8),
        name="mix_local",
    )(in_hbm(field), weight, bias, *more)


def back_kernel(first, chunk, field_ref, weight_ref, delta_ref, out_ref, grad_ref, held, sems):
    blocks, channels, block, width = held.shape
    copies = fetch_rows(field_ref, held, sems, first, block)
    weight = spread_weight(weight_ref[...]) * 0.5
    grad = jnp.zeros(grad_ref.shape, F32)
    for i, copy in enumerate(copies):
        copy.wait()
        rows = slice(first + i * block, first + (i + 1) * block)
        for start in range(0, width, chunk):
            columns = pl.ds(start, chunk)
            field = held[i, :, :, columns].astype(F32)
            delta = delta_ref[:, rows, columns].astype(F32)
            parts = []
            for group in range(0, block, GROUP):
                delta_group = group_rows(delta, group)
                grad += dot_last(group_rows(field, group), delta_group)
                parts.append(dot(weight, delta_group).reshape(channels, GROUP, chunk))
            out_ref[:, rows, columns] = jnp.concatenate(parts, axis=1).astype(BF16)
    grad_ref[...] = grad * 0.5


def mix_back_local(field, weight, out, first, count, block=16, chunk=512):
    size = field.shape[0] * GROUP
    return pl.pallas_call(
        functools.partial(back_kernel, first, chunk),
        in_specs=[HBM, VMEM, VMEM],
        out_specs=[VMEM] * 2,
        out_shape=[pltpu.VMEM(field.shape, BF16), jax.ShapeDtypeStruct((size, size), F32)],
        scratch_shapes=row_scratch(field, count, block),
        input_output_aliases={2: 0},
        compiler_params=params(14),
        name="mix_back_local",
    )(in_hbm(field), weight, in_vmem(out))


def load_modes(modes, first_ref, second_ref, scale=1.0):
    half = modes.shape[0] // 2
    modes[:half] = first_ref[:half].astype(F32) * scale
    modes[half:] = second_ref[:half].astype(F32) * scale


def delta_kernel(
    block, chunk, local_ref, target_ref, first_ref, second_ref, basis_ref, basis_t_ref, tables_ref,
    delta_ref, send_ref, keep_ref, sums_ref, mixed, modes, held, sems,
):
    channels, rows, width = local_ref.shape
    steps = channels // block
    slots = held.shape[0]
    copies = [
        pltpu.make_async_copy(target_ref.at[pl.ds(i * block, block)], held.at[i % slots], sems.at[i % slots])
        for i in range(steps)
    ]
    for copy in copies[: slots - 1]:
        copy.start()
    load_modes(mixed, first_ref, second_ref, SCALE)

    def spectra_of(step):
        first = step * block
        return jnp.concatenate([column_synthesis(mixed, first + i, channels, tables_ref) for i in range(block)], axis=0)

    def finish(product, step):
        store_modes(product, step * block, block, tables_ref, modes)
        sums = jnp.sum(product.reshape(block, rows, LANES), axis=1)
        sums_ref[pl.ds(step * block, block), :] = sums

    product = None
    spectra = spectra_of(0)
    for step in range(steps):
        if step + slots - 1 < steps:
            copies[step + slots - 1].start()
        copies[step].wait()
        here, slot = pl.ds(step * block, block), step % slots
        before, product = product, jnp.zeros((block * rows, LANES), F32)
        for start in range(0, width, chunk):
            columns = pl.ds(start, chunk)
            local = local_ref[here, :, columns].reshape(block * rows, chunk).astype(F32)
            target = held[slot, :, :, columns].reshape(block * rows, chunk)
            delta = twice_delta(dot(spectra, basis_ref[:, columns]) + local, target)
            delta_ref[here, :, columns] = delta.reshape(block, rows, chunk)
            product += dot(delta, basis_t_ref[columns, :])
        product *= 0.5
        if before is not None:
            finish(before, step - 1)
        if step + 1 < steps:
            spectra = spectra_of(step + 1)
    finish(product, steps - 1)
    emit_halves(modes, send_ref, keep_ref)


def make_delta(local, target, first, second, basis, basis_t, tables, block=4, chunk=1024, slots=3):
    channels, rows, width = local.shape
    scratch = pltpu.VMEM((KY * channels, LANES), F32)
    return pl.pallas_call(
        functools.partial(delta_kernel, block, chunk),
        in_specs=[VMEM, HBM] + [VMEM] * 5,
        out_specs=[VMEM] * 4,
        out_shape=[pltpu.VMEM(local.shape, BF16)]
        + half_shapes(channels)
        + [jax.ShapeDtypeStruct((channels, LANES), F32)],
        scratch_shapes=[
            scratch, scratch, pltpu.VMEM((slots, block, rows, width), BF16), pltpu.SemaphoreType.DMA((slots,))
        ],
        input_output_aliases={0: 0},
        compiler_params=params(18),
        name="make_delta",
    )(in_vmem(local), in_hbm(target), first, second, basis, basis_t, tables)


def synthesis_kernel(
    block, chunk, local_ref, first_ref, second_ref, basis_ref, tables_ref, sum_ref, out_ref, modes, sems
):
    channels, rows, width = local_ref.shape
    steps = channels // block
    load_modes(modes, first_ref, second_ref)

    def spectra_of(step):
        first = step * block
        return jnp.concatenate([column_synthesis(modes, first + i, channels, tables_ref) for i in range(block)], axis=0)

    copies = []
    spectra = spectra_of(0)
    for step in range(steps):
        here = pl.ds(step * block, block)
        for start in range(0, width, chunk):
            columns = pl.ds(start, chunk)
            local = local_ref[here, :, columns].reshape(block * rows, chunk).astype(F32)
            value = dot(spectra, basis_ref[:, columns]) + local
            sum_ref[here, :, columns] = value.astype(BF16).reshape(block, rows, chunk)
        copies.append(pltpu.make_async_copy(sum_ref.at[here], out_ref.at[here], sems.at[step]))
        copies[step].start()
        if step + 1 < steps:
            spectra = spectra_of(step + 1)
    for copy in copies:
        copy.wait()


def synthesise(local, first, second, basis, tables, block=4, chunk=1024):
    channels = local.shape[0]
    return pl.pallas_call(
        functools.partial(synthesis_kernel, block, chunk),
        in_specs=[VMEM] * 5,
        out_specs=[VMEM, HBM],
        out_shape=[pltpu.VMEM(local.shape, BF16), jax.ShapeDtypeStruct(local.shape, BF16)],
        scratch_shapes=[pltpu.VMEM((KY * channels, LANES), F32), pltpu.SemaphoreType.DMA((channels // block,))],
        input_output_aliases={0: 0},
        compiler_params=params(8),
        name="synthesise",
    )(in_vmem(local), first, second, basis, tables)[1]


def sum_parts(refs):
    return functools.reduce(lambda a, b: a + b, [ref[...].astype(F32) for ref in refs])


def mix_modes_kernel(count, channels, *refs):
    parts, (weight_ref, gain_ref, mixed_ref, modes_ref) = refs[:-4], refs[-4:]
    modes_ref[...] = sum_parts(parts)
    real = real_lanes((channels, LANES))
    for q in range(count):
        rows = slice(q * channels, (q + 1) * channels)
        modes = modes_ref[rows]
        other = swap_halves(modes)
        first, second = jnp.where(real, modes, other), jnp.where(real, other, -modes)
        direct = jnp.zeros((channels, LANES), F32)
        crossed = jnp.zeros((channels, LANES), F32)
        for c in range(channels):
            weight = weight_ref[q, c]
            direct += first[c : c + 1] * weight
            crossed += second[c : c + 1] * weight
        mixed_ref[rows] = ((direct + swap_halves(crossed)) * gain_ref[q : q + 1]).astype(BF16)


def mix_modes(parts, weight, gain):
    count, channels = weight.shape[:2]
    return pl.pallas_call(
        functools.partial(mix_modes_kernel, count, channels),
        out_shape=[
            jax.ShapeDtypeStruct((count * channels, LANES), BF16),
            jax.ShapeDtypeStruct((count * channels, LANES), F32),
        ],
        compiler_params=params(3),
        name="mix_modes",
    )(*parts, weight, gain)


def split_value(value):
    parts = []
    for _ in range(3):
        part = value.astype(BF16)
        value = value - part.astype(F32)
        parts.append(part)
    return jnp.concatenate(parts, axis=0)


def join_value(parts):
    size = parts.shape[0] // 3
    parts = parts.astype(F32)
    return (parts[:size] + parts[size : 2 * size]) + parts[2 * size :]


def tree(values):
    while len(values) > 1:
        values = [values[i] + values[i + 1] for i in range(0, len(values), 2)]
    return values[0]


def shared_terms(total, sums, first_lane, factor):
    channels, size = sums.shape[0], total.shape[0]
    total = jnp.where(same_row(size), total, 0.0)
    total = jnp.sum(total.reshape(channels, GROUP, size), axis=1)
    wide = lax.broadcasted_iota(jnp.int32, (LANES, size), 1) // GROUP
    pick = (wide == lax.broadcasted_iota(jnp.int32, (LANES, size), 0)).astype(F32)
    weight = lax.dot_general(
        total, pick, (((1,), (1,)), ((), ())), precision=lax.Precision.HIGHEST, preferred_element_type=F32
    )
    bias = jnp.sum(sums * first_lane, axis=1, keepdims=True) * factor
    lane = lax.broadcasted_iota(jnp.int32, weight.shape, 1)
    return jnp.where(lane == channels, bias, weight)


def mix_back_kernel(count, channels, factor, terms, *refs):
    parts, grads, (sums_ref, lane_ref, weight_ref, gain_ref, back_ref, delta_ref) = (
        refs[: -6 - terms], refs[-6 - terms : -6], refs[-6:]
    )
    delta_ref[...] = sum_parts(parts)
    real = real_lanes((channels, LANES))
    for q in range(count):
        rows = slice(q * channels, (q + 1) * channels)
        delta = delta_ref[rows] * gain_ref[q : q + 1]
        delta_ref[rows] = delta
        other = swap_halves(delta)
        first, second = jnp.where(real, delta, -other), jnp.where(real, other, delta)
        direct, crossed = [], []
        for c in range(channels):
            weight = weight_ref[q, c]
            direct.append(jnp.sum(first * weight, axis=0, keepdims=True))
            crossed.append(jnp.sum(second * weight, axis=0, keepdims=True))
        direct, crossed = jnp.concatenate(direct, axis=0), jnp.concatenate(crossed, axis=0)
        back_ref[rows] = (direct + swap_halves(crossed)).astype(BF16)
    shared = shared_terms(sum_parts(grads), sums_ref[...], lane_ref[...], factor)
    back_ref[count * channels :] = split_value(shared)


def mix_back(parts, grads, sums, first_lane, weight, gain, factor):
    count, channels = weight.shape[:2]
    return pl.pallas_call(
        functools.partial(mix_back_kernel, count, channels, factor, len(grads)),
        out_shape=[
            jax.ShapeDtypeStruct(((count + 3) * channels, LANES), BF16),
            jax.ShapeDtypeStruct((count * channels, LANES), F32),
        ],
        compiler_params=params(6),
        name="mix_back",
    )(*parts, *grads, sums, first_lane, weight, gain)


def join_kernel(extra, *refs):
    parts, out_ref = refs[:-1], refs[-1]
    size = parts[0].shape[0] - extra
    for i, part in enumerate(parts):
        out_ref[i * size : (i + 1) * size] = part[:size]
    if extra:
        out_ref[len(parts) * size :] = split_value(tree([join_value(part[size:]) for part in parts]))


def join(parts, extra):
    rows = (parts[0].shape[0] - extra) * len(parts) + extra
    return pl.pallas_call(
        functools.partial(join_kernel, extra),
        out_shape=jax.ShapeDtypeStruct((rows, LANES), BF16),
        compiler_params=params(4),
        name="join",
    )(*parts)


def grad_kernel(count, channels, modes_ref, delta_ref, grad_ref):
    real = real_lanes((channels, LANES))
    for q in range(count):
        rows = slice(q * channels, (q + 1) * channels)
        modes, delta = modes_ref[rows], delta_ref[rows]
        other, delta_other = swap_halves(modes), swap_halves(delta)
        first, second = jnp.where(real, modes, other), jnp.where(real, other, -modes)
        for c in range(channels):
            grad_ref[q, c] = first[c : c + 1] * delta + second[c : c + 1] * delta_other


def mode_grad(modes, delta, count, channels):
    return pl.pallas_call(
        functools.partial(grad_kernel, count, channels),
        out_shape=jax.ShapeDtypeStruct((count, channels, channels, LANES), F32),
        compiler_params=params(6),
        name="mode_grad",
    )(modes, delta)


def per_device(devices, inputs, target, spectral_weight, local_weight, bias_term):
    samples, channels, rows, width = inputs.shape
    assert samples == 1
    field, target = inputs[0], target[0]
    height = rows * devices
    count = spectral_weight.shape[0]
    device = lax.axis_index("space")
    far = devices // 4

    place = np.arange(KY) // count
    offset = place // (2 * far) + 2 * (place // far % 2) + 4 * (place % far)
    order = (device ^ jnp.asarray(offset, jnp.int32)) * count + jnp.asarray(np.arange(KY) % count, jnp.int32)
    source = jnp.concatenate([order, order + KY])
    pick = (jnp.arange(LANES, dtype=jnp.int32)[:, None] == source[None, :]).astype(BF16)
    basis_table = row_basis_table(height, width)
    basis_t = dot(jnp.asarray(basis_table.T.copy()), pick).astype(BF16)
    tables = lax.dynamic_slice_in_dim(jnp.asarray(column_tables(height)), device * rows, rows, 0)
    mode_index = device * count + jnp.arange(count, dtype=jnp.int32)
    gain = jnp.broadcast_to(jnp.where(mode_index == 0, 1.0, 2.0).astype(F32)[:, None], (count, LANES))

    def exchange(value, mask):
        return lax.ppermute(value, "space", [(i, i ^ mask) for i in range(devices)])

    barrier = lax.optimization_barrier

    def beside(sent, received, work, state):
        if work is None:
            return received, state
        sent, state = barrier((sent, state))
        return barrier((received, work(state)))

    def reduce_modes(send, keep, work, state):
        received = exchange(send, 1).astype(F32)
        half = keep.shape[0] // 2
        send = (keep[half:] + received[half:]).astype(BF16)
        keep = keep[:half] + received[:half]
        received, state = beside(send, exchange(send, 2), work[0], state)
        total = keep + received.astype(F32)
        size = total.shape[0] // far
        pieces = [total[i * size : (i + 1) * size].astype(BF16) for i in range(1, far)]
        received, state = beside(pieces, [exchange(p, 4 * (i + 1)) for i, p in enumerate(pieces)], work[1], state)
        return [total[:size]] + received, state

    def gather_modes(own, extra, work, state):
        received, state = beside(own, [exchange(own, 4 * i) for i in range(1, far)], work[0], state)
        part = join([own] + received, extra)
        received, state = beside(part, exchange(part, 2), work[1], state)
        part = join([part, received], extra)
        return part, exchange(part, 1), state

    send, keep = analyse(field, basis_t, tables)
    bias = bias_term[:, None]
    splits = 4 if rows % 64 == 0 else 1
    step = rows // splits

    def local_work(i):
        if i >= splits:
            return None
        return lambda state: mix_local(field, forward_weight, bias, state, i * step, step)

    forward_weight = local_weight.T
    parts, state = reduce_modes(send, keep, [local_work(0), local_work(1)], None)
    mixed, modes = mix_modes(parts, spectral_weight, gain)
    first, second, local = gather_modes(mixed, 0, [local_work(2), local_work(3)], state)
    basis = lax.dot_general(pick, jnp.asarray(basis_table), (((0,), (0,)), ((), ())), preferred_element_type=F32)
    basis = basis.astype(BF16)
    delta, send, keep, sums = make_delta(local, target, first, second, basis, basis_t, tables)

    back_splits = min(splits, 2)
    back_step = rows // back_splits

    def back_work(i):
        if i >= back_splits:
            return None

        def work(state):
            out, grads = state
            out, grad = mix_back_local(field, local_weight, out, i * back_step, back_step)
            return out, grads + [grad]

        return work

    parts, (back_local, grads) = reduce_modes(send, keep, [back_work(0), back_work(1)], (delta, []))
    factor = math.sqrt(height * width)
    first_lane = pick[:1].astype(F32)
    back, delta_modes = mix_back(parts, grads, sums, first_lane, spectral_weight, gain, factor)
    extra = 3 * channels
    first, second, grad_spectral = gather_modes(
        back, extra, [lambda pair: mode_grad(*pair, count, channels), None], (modes, delta_modes)
    )
    grad_input = synthesise(back_local, first, second, basis, tables)
    shared = join_value(first[-extra:]) + join_value(second[-extra:])
    shared = shared / (samples * height * width)
    return (grad_input[None], grad_spectral, shared[:, :channels], shared[:, channels])


def solution(mesh):
    return jax.shard_map(
        functools.partial(per_device, mesh.shape["space"]),
        mesh=mesh,
        in_specs=(
            P("dom", None, "space", None),
            P("dom", None, "space", None),
            P("space", None, None, None),
            P(),
            P(),
        ),
        out_specs=(
            P("dom", None, "space", None),
            P("space", "dom", None, None),
            P("dom", None),
            P("dom"),
        ),
        check_vma=False,
    )
```

```python
import functools
import math

import jax
import jax.numpy as jnp
import ml_dtypes
import numpy as np
from jax import lax
from jax.experimental import pallas as pl
from jax.experimental.pallas import tpu as pltpu
from jax.sharding import PartitionSpec as P

KX = 64
KY = 64
LANES = 2 * KX
GROUP = 8
F32 = jnp.float32
BF16 = jnp.bfloat16
SCALE = math.sqrt(0.5)

dot = functools.partial(jnp.dot, preferred_element_type=F32)


def dot_last(a, b):
    return lax.dot_general(a, b, (((1,), (1,)), ((), ())), preferred_element_type=F32)


def params(mib):
    return pltpu.CompilerParams(vmem_limit_bytes=mib * 2**20)


def row_basis_table(height, width):
    angles = 2.0 * np.pi / width * (np.arange(KY)[:, None] * np.arange(width)[None, :] % width)
    factor = 1.0 / math.sqrt(height * width)
    table = np.concatenate([np.cos(angles) * factor, -np.sin(angles) * factor])
    return table.astype(np.float32).astype(ml_dtypes.bfloat16)


def column_tables(height):
    index = np.arange(KX)
    frequency = np.where(index < KX // 2, index, index + height - KX)
    angles = 2.0 * np.pi / height * (np.arange(height)[:, None] * frequency[None, :] % height)
    cosines, sines = np.cos(angles), np.sin(angles)

    def parts(table):
        high = table.astype(np.float32).astype(ml_dtypes.bfloat16)
        low = (table - high.astype(np.float64)).astype(np.float32).astype(ml_dtypes.bfloat16)
        return high, low

    synthesis = parts(np.concatenate([cosines, sines], axis=1))
    analysis = parts(np.concatenate([cosines, -sines, sines, cosines], axis=1))
    return np.concatenate(synthesis + analysis, axis=1)


def swap_halves(value):
    return pltpu.roll(value, LANES // 2, 1)


def real_lanes(shape):
    return lax.broadcasted_iota(jnp.int32, shape, 1) < LANES // 2


def column_analysis(row_modes, tables_ref):
    rows = row_modes[0].shape[0]
    first, second = LANES * 2, LANES * 3
    high = [tables_ref[:, first : first + LANES], tables_ref[:, second : second + LANES]]
    low = [tables_ref[:, first + 2 * LANES : first + 3 * LANES], tables_ref[:, second + 2 * LANES : second + 3 * LANES]]
    flipped = [value.T for value in row_modes]
    parts = [[value[:KY] for value in flipped], [value[KY:] for value in flipped]]
    parts = [jnp.concatenate(part, axis=0) for part in parts]
    if rows % 128 == 0:
        parts = [jnp.concatenate(parts, axis=1)]
        high = [jnp.concatenate(high, axis=0)]
        low = [jnp.concatenate(low, axis=0)]
    total = 0.0
    for part, table_high, table_low in zip(parts, high, low):
        part_high = part.astype(BF16)
        part_low = (part - part_high.astype(F32)).astype(BF16)
        total += dot(part_high, table_high) + dot(part_low, table_high) + dot(part_high, table_low)
    return [total[i * KY : (i + 1) * KY] for i in range(len(row_modes))]


def column_synthesis(modes_ref, channel, channels, tables_ref):
    modes = modes_ref[pl.ds(channel, KY, stride=channels), :]
    real = real_lanes(modes.shape)
    both = jnp.concatenate([jnp.where(real, modes, -modes), swap_halves(modes)], axis=0).astype(BF16)
    both = jnp.concatenate([both, both], axis=1)
    return dot_last(tables_ref[:, : 2 * LANES], both).astype(BF16)


def twice_delta(value, target):
    cdf = 1.0 + lax.erf(value)
    density = jnp.exp2(value * (value * -math.log2(math.e))) * (2.0 / math.sqrt(math.pi))
    value, cdf, density = value.astype(BF16), cdf.astype(BF16), density.astype(BF16)
    return (value * cdf * BF16(SCALE) - target) * (cdf + value * density)


def store_modes(product, first, block, tables_ref, modes):
    rows = product.shape[0] // block
    channels = modes.shape[0] // KY
    parts = column_analysis([product[i * rows : (i + 1) * rows] for i in range(block)], tables_ref)
    for i, part in enumerate(parts):
        modes[pl.ds(first + i, KY, stride=channels), :] = part


def emit_halves(modes, send_ref, keep_ref):
    half = modes.shape[0] // 2
    keep_ref[...] = modes[:half]
    send_ref[...] = modes[half:].astype(BF16)


VMEM = pl.BlockSpec(memory_space=pltpu.VMEM)
HBM = pl.BlockSpec(memory_space=pl.ANY)


def in_vmem(array):
    return pltpu.with_memory_space_constraint(array, pltpu.VMEM)


def in_hbm(array):
    return pltpu.with_memory_space_constraint(array, pltpu.HBM)


def half_shapes(channels):
    half = KY // 2 * channels
    return [jax.ShapeDtypeStruct((half, LANES), BF16), jax.ShapeDtypeStruct((half, LANES), F32)]


def analysis_kernel(block, field_ref, basis_ref, tables_ref, send_ref, keep_ref, held_ref, modes, sems):
    channels, rows, width = field_ref.shape
    copies = [pltpu.make_async_copy(field_ref.at[i], held_ref.at[i], sems.at[i]) for i in range(channels)]
    for copy in copies:
        copy.start()
    product = None
    for start in range(0, channels + block, block):
        before, product = product, None
        if start < channels:
            for copy in copies[start : start + block]:
                copy.wait()
            product = dot(held_ref[pl.ds(start, block)].reshape(block * rows, width), basis_ref[...])
        if before is not None:
            store_modes(before, start - block, block, tables_ref, modes)
    emit_halves(modes, send_ref, keep_ref)


def analyse(field, basis_t, tables, block=2):
    channels = field.shape[0]
    return pl.pallas_call(
        functools.partial(analysis_kernel, block),
        in_specs=[HBM, VMEM, VMEM],
        out_specs=[VMEM] * 2,
        out_shape=half_shapes(channels),
        scratch_shapes=[pltpu.VMEM(field.shape, BF16), pltpu.VMEM((KY * channels, LANES), F32), pltpu.SemaphoreType.DMA((channels,))],
        compiler_params=params(24),
        name="analyse",
    )(in_hbm(field), basis_t, tables)


def group_rows(value, start):
    channels, _, width = value.shape
    return value[:, start : start + GROUP, :].reshape(channels * GROUP, width).astype(BF16)


def picks(channels):
    size = channels * GROUP
    wide = lax.broadcasted_iota(jnp.int32, (channels, size), 1) // GROUP
    return (wide == lax.broadcasted_iota(jnp.int32, (channels, size), 0)).astype(BF16)


def same_row(size):
    row = lax.broadcasted_iota(jnp.int32, (size, size), 0) % GROUP
    return row == lax.broadcasted_iota(jnp.int32, (size, size), 1) % GROUP


def spread_weight(weight):
    pick = picks(weight.shape[0])
    wide = dot(weight, pick).astype(BF16)
    full = lax.dot_general(pick, wide, (((0,), (0,)), ((), ())), preferred_element_type=F32)
    return jnp.where(same_row(pick.shape[1]), full, 0.0).astype(BF16)


def fetch_rows(field_ref, held, sems, first, block):
    copies = [
        pltpu.make_async_copy(field_ref.at[:, pl.ds(first + i * block, block)], held.at[i], sems.at[i])
        for i in range(held.shape[0])
    ]
    for copy in copies:
        copy.start()
    return copies


def local_kernel(first, chunk, field_ref, weight_ref, bias_ref, *rest):
    out_ref, held, sems = rest[-3:]
    blocks, channels, block, width = held.shape
    copies = fetch_rows(field_ref, held, sems, first, block)
    weight = spread_weight(weight_ref[...])
    bias = lax.dot_general(
        picks(channels).astype(F32), bias_ref[...], (((0,), (0,)), ((), ())),
        precision=lax.Precision.HIGHEST, preferred_element_type=F32,
    )
    for i, copy in enumerate(copies):
        copy.wait()
        rows = slice(first + i * block, first + (i + 1) * block)
        for start in range(0, width, chunk):
            columns = pl.ds(start, chunk)
            field = held[i, :, :, columns].astype(F32)
            parts = []
            for group in range(0, block, GROUP):
                part = (dot(weight, group_rows(field, group)) + bias) * SCALE
                parts.append(part.reshape(channels, GROUP, chunk))
            out_ref[:, rows, columns] = jnp.concatenate(parts, axis=1).astype(BF16)


def mix_local(field, weight, bias, out, first, count, block=16, chunk=512):
    more = [] if out is None else [in_vmem(out)]
    return pl.pallas_call(
        functools.partial(local_kernel, first, chunk),
        in_specs=[HBM] + [VMEM] * (2 + len(more)),
        out_specs=VMEM,
        out_shape=pltpu.VMEM(field.shape, BF16),
        scratch_shapes=row_scratch(field, count, block, count // block),
        input_output_aliases={3: 0} if more else {},
        compiler_params=params(8),
        name="mix_local",
    )(in_hbm(field), weight, bias, *more)


def row_copies(field_ref, held, sems, first, count):
    slots, _, block, _ = held.shape
    return [
        pltpu.make_async_copy(
            field_ref.at[:, pl.ds(first + i * block, block)], held.at[i % slots], sems.at[i % slots]
        )
        for i in range(count // block)
    ]


def row_scratch(field, count, block, slots):
    channels, _, width = field.shape
    slots = min(slots, count // block)
    return [pltpu.VMEM((slots, channels, block, width), BF16), pltpu.SemaphoreType.DMA((slots,))]


def weight_kernel(first, count, chunk, field_ref, delta_ref, _, grad_ref, held, sems):
    width = field_ref.shape[2]
    slots, _, block, _ = held.shape
    copies = row_copies(field_ref, held, sems, first, count)
    for copy in copies[:slots]:
        copy.start()
    grad = jnp.zeros(grad_ref.shape, F32)
    for i, copy in enumerate(copies):
        copy.wait()
        here = slice(first + i * block, first + (i + 1) * block)
        for start in range(0, width, chunk):
            columns = pl.ds(start, chunk)
            field = held[i % slots, :, :, columns].astype(F32)
            delta = delta_ref[:, here, columns].astype(F32)
            for group in range(0, block, GROUP):
                grad += dot_last(group_rows(field, group), group_rows(delta, group))
        if i + slots < len(copies):
            copies[i + slots].start()
    grad_ref[...] = grad * 0.5


def weight_grad(field, delta, first, count, block=16, chunk=1024):
    channels = field.shape[0]
    return pl.pallas_call(
        functools.partial(weight_kernel, first, count, chunk),
        in_specs=[HBM, VMEM],
        out_specs=[VMEM] * 2,
        out_shape=[pltpu.VMEM(delta.shape, BF16), jax.ShapeDtypeStruct((channels * GROUP,) * 2, F32)],
        input_output_aliases={1: 0},
        scratch_shapes=row_scratch(field, count, block, 3),
        compiler_params=params(10),
        name="weight_grad",
    )(in_hbm(field), in_vmem(delta))


def back_kernel(first, count, block, chunk, weight_ref, delta_ref, out_ref):
    channels, _, width = delta_ref.shape
    weight = spread_weight(weight_ref[...]) * 0.5
    for row in range(first, first + count, block):
        here = slice(row, row + block)
        for start in range(0, width, chunk):
            columns = pl.ds(start, chunk)
            delta = delta_ref[:, here, columns].astype(F32)
            parts = []
            for group in range(0, block, GROUP):
                parts.append(dot(weight, group_rows(delta, group)).reshape(channels, GROUP, chunk))
            out_ref[:, here, columns] = jnp.concatenate(parts, axis=1).astype(BF16)


def mix_back_local(weight, delta, first, count, block=16, chunk=512):
    return pl.pallas_call(
        functools.partial(back_kernel, first, count, block, chunk),
        in_specs=[VMEM, VMEM],
        out_specs=VMEM,
        out_shape=pltpu.VMEM(delta.shape, BF16),
        input_output_aliases={1: 0},
        compiler_params=params(8),
        name="mix_back_local",
    )(weight, in_vmem(delta))


def load_modes(modes, first_ref, second_ref, scale=1.0):
    half = modes.shape[0] // 2
    modes[:half] = first_ref[:half].astype(F32) * scale
    modes[half:] = second_ref[:half].astype(F32) * scale


def delta_kernel(
    block, chunk, local_ref, target_ref, first_ref, second_ref, basis_ref, basis_t_ref, tables_ref,
    delta_ref, send_ref, keep_ref, sums_ref, mixed, modes, held, sems,
):
    channels, rows, width = local_ref.shape
    steps = channels // block
    slots = held.shape[0]
    copies = [
        pltpu.make_async_copy(target_ref.at[pl.ds(i * block, block)], held.at[i % slots], sems.at[i % slots])
        for i in range(steps)
    ]
    for copy in copies[: slots - 1]:
        copy.start()
    load_modes(mixed, first_ref, second_ref, SCALE)

    def spectra_of(step):
        first = step * block
        return jnp.concatenate([column_synthesis(mixed, first + i, channels, tables_ref) for i in range(block)], axis=0)

    def finish(product, step):
        store_modes(product, step * block, block, tables_ref, modes)
        sums = jnp.sum(product.reshape(block, rows, LANES), axis=1)
        sums_ref[pl.ds(step * block, block), :] = sums

    product = None
    spectra = spectra_of(0)
    for step in range(steps):
        if step + slots - 1 < steps:
            copies[step + slots - 1].start()
        copies[step].wait()
        here, slot = pl.ds(step * block, block), step % slots
        before, product = product, jnp.zeros((block * rows, LANES), F32)
        for start in range(0, width, chunk):
            columns = pl.ds(start, chunk)
            local = local_ref[here, :, columns].reshape(block * rows, chunk).astype(F32)
            target = held[slot, :, :, columns].reshape(block * rows, chunk)
            delta = twice_delta(dot(spectra, basis_ref[:, columns]) + local, target)
            delta_ref[here, :, columns] = delta.reshape(block, rows, chunk)
            product += dot(delta, basis_t_ref[columns, :])
        product *= 0.5
        if before is not None:
            finish(before, step - 1)
        if step + 1 < steps:
            spectra = spectra_of(step + 1)
    finish(product, steps - 1)
    emit_halves(modes, send_ref, keep_ref)


def make_delta(local, target, first, second, basis, basis_t, tables, block=4, chunk=1024, slots=3):
    channels, rows, width = local.shape
    scratch = pltpu.VMEM((KY * channels, LANES), F32)
    return pl.pallas_call(
        functools.partial(delta_kernel, block, chunk),
        in_specs=[VMEM, HBM] + [VMEM] * 5,
        out_specs=[VMEM] * 4,
        out_shape=[pltpu.VMEM(local.shape, BF16)]
        + half_shapes(channels)
        + [jax.ShapeDtypeStruct((channels, LANES), F32)],
        scratch_shapes=[
            scratch, scratch, pltpu.VMEM((slots, block, rows, width), BF16), pltpu.SemaphoreType.DMA((slots,))
        ],
        input_output_aliases={0: 0},
        compiler_params=params(18),
        name="make_delta",
    )(in_vmem(local), in_hbm(target), first, second, basis, basis_t, tables)


def synthesis_kernel(
    block, chunk, local_ref, first_ref, second_ref, basis_ref, tables_ref, sum_ref, out_ref, modes, sems
):
    channels, rows, width = local_ref.shape
    steps = channels // block
    load_modes(modes, first_ref, second_ref)

    def spectra_of(step):
        first = step * block
        return jnp.concatenate([column_synthesis(modes, first + i, channels, tables_ref) for i in range(block)], axis=0)

    copies = []
    spectra = spectra_of(0)
    for step in range(steps):
        here = pl.ds(step * block, block)
        for start in range(0, width, chunk):
            columns = pl.ds(start, chunk)
            local = local_ref[here, :, columns].reshape(block * rows, chunk).astype(F32)
            value = dot(spectra, basis_ref[:, columns]) + local
            sum_ref[here, :, columns] = value.astype(BF16).reshape(block, rows, chunk)
        copies.append(pltpu.make_async_copy(sum_ref.at[here], out_ref.at[here], sems.at[step]))
        copies[step].start()
        if step + 1 < steps:
            spectra = spectra_of(step + 1)
    for copy in copies:
        copy.wait()


def synthesise(local, first, second, basis, tables, block=4, chunk=1024):
    channels = local.shape[0]
    return pl.pallas_call(
        functools.partial(synthesis_kernel, block, chunk),
        in_specs=[VMEM] * 5,
        out_specs=[VMEM, HBM],
        out_shape=[pltpu.VMEM(local.shape, BF16), jax.ShapeDtypeStruct(local.shape, BF16)],
        scratch_shapes=[pltpu.VMEM((KY * channels, LANES), F32), pltpu.SemaphoreType.DMA((channels // block,))],
        input_output_aliases={0: 0},
        compiler_params=params(8),
        name="synthesise",
    )(in_vmem(local), first, second, basis, tables)[1]


def sum_parts(refs):
    return functools.reduce(lambda a, b: a + b, [ref[...].astype(F32) for ref in refs])


def mix_modes_kernel(count, channels, *refs):
    parts, (weight_ref, gain_ref, mixed_ref, modes_ref) = refs[:-4], refs[-4:]
    modes_ref[...] = sum_parts(parts)
    real = real_lanes((channels, LANES))
    for q in range(count):
        rows = slice(q * channels, (q + 1) * channels)
        modes = modes_ref[rows]
        other = swap_halves(modes)
        first, second = jnp.where(real, modes, other), jnp.where(real, other, -modes)
        direct = jnp.zeros((channels, LANES), F32)
        crossed = jnp.zeros((channels, LANES), F32)
        for c in range(channels):
            weight = weight_ref[q, c]
            direct += first[c : c + 1] * weight
            crossed += second[c : c + 1] * weight
        mixed_ref[rows] = ((direct + swap_halves(crossed)) * gain_ref[q : q + 1]).astype(BF16)


def mix_modes(parts, weight, gain):
    count, channels = weight.shape[:2]
    return pl.pallas_call(
        functools.partial(mix_modes_kernel, count, channels),
        out_shape=[
            jax.ShapeDtypeStruct((count * channels, LANES), BF16),
            jax.ShapeDtypeStruct((count * channels, LANES), F32),
        ],
        compiler_params=params(3),
        name="mix_modes",
    )(*parts, weight, gain)


def split_value(value):
    parts = []
    for _ in range(3):
        part = value.astype(BF16)
        value = value - part.astype(F32)
        parts.append(part)
    return jnp.concatenate(parts, axis=0)


def join_value(parts):
    size = parts.shape[0] // 3
    parts = parts.astype(F32)
    return (parts[:size] + parts[size : 2 * size]) + parts[2 * size :]


def tree(values):
    while len(values) > 1:
        values = [values[i] + values[i + 1] for i in range(0, len(values), 2)]
    return values[0]


def shared_terms(total, sums, first_lane, factor):
    channels, size = sums.shape[0], total.shape[0]
    total = jnp.where(same_row(size), total, 0.0)
    total = jnp.sum(total.reshape(channels, GROUP, size), axis=1)
    wide = lax.broadcasted_iota(jnp.int32, (LANES, size), 1) // GROUP
    pick = (wide == lax.broadcasted_iota(jnp.int32, (LANES, size), 0)).astype(F32)
    weight = lax.dot_general(
        total, pick, (((1,), (1,)), ((), ())), precision=lax.Precision.HIGHEST, preferred_element_type=F32
    )
    bias = jnp.sum(sums * first_lane, axis=1, keepdims=True) * factor
    lane = lax.broadcasted_iota(jnp.int32, weight.shape, 1)
    return jnp.where(lane == channels, bias, weight)


def mix_back_kernel(count, channels, factor, terms, *refs):
    parts, grads, (sums_ref, lane_ref, weight_ref, gain_ref, back_ref, delta_ref) = (
        refs[: -6 - terms], refs[-6 - terms : -6], refs[-6:]
    )
    delta_ref[...] = sum_parts(parts)
    real = real_lanes((channels, LANES))
    for q in range(count):
        rows = slice(q * channels, (q + 1) * channels)
        delta = delta_ref[rows] * gain_ref[q : q + 1]
        delta_ref[rows] = delta
        other = swap_halves(delta)
        first, second = jnp.where(real, delta, -other), jnp.where(real, other, delta)
        direct, crossed = [], []
        for c in range(channels):
            weight = weight_ref[q, c]
            direct.append(jnp.sum(first * weight, axis=0, keepdims=True))
            crossed.append(jnp.sum(second * weight, axis=0, keepdims=True))
        direct, crossed = jnp.concatenate(direct, axis=0), jnp.concatenate(crossed, axis=0)
        back_ref[rows] = (direct + swap_halves(crossed)).astype(BF16)
    shared = shared_terms(sum_parts(grads), sums_ref[...], lane_ref[...], factor)
    back_ref[count * channels :] = split_value(shared)


def mix_back(parts, grads, sums, first_lane, weight, gain, factor):
    count, channels = weight.shape[:2]
    return pl.pallas_call(
        functools.partial(mix_back_kernel, count, channels, factor, len(grads)),
        out_shape=[
            jax.ShapeDtypeStruct(((count + 3) * channels, LANES), BF16),
            jax.ShapeDtypeStruct((count * channels, LANES), F32),
        ],
        compiler_params=params(6),
        name="mix_back",
    )(*parts, *grads, sums, first_lane, weight, gain)


def join_kernel(extra, *refs):
    parts, out_ref = refs[:-1], refs[-1]
    size = parts[0].shape[0] - extra
    for i, part in enumerate(parts):
        out_ref[i * size : (i + 1) * size] = part[:size]
    if extra:
        out_ref[len(parts) * size :] = split_value(tree([join_value(part[size:]) for part in parts]))


def join(parts, extra):
    rows = (parts[0].shape[0] - extra) * len(parts) + extra
    return pl.pallas_call(
        functools.partial(join_kernel, extra),
        out_shape=jax.ShapeDtypeStruct((rows, LANES), BF16),
        compiler_params=params(4),
        name="join",
    )(*parts)


def grad_kernel(count, channels, modes_ref, delta_ref, grad_ref):
    real = real_lanes((channels, LANES))
    for q in range(count):
        rows = slice(q * channels, (q + 1) * channels)
        modes, delta = modes_ref[rows], delta_ref[rows]
        other, delta_other = swap_halves(modes), swap_halves(delta)
        first, second = jnp.where(real, modes, other), jnp.where(real, other, -modes)
        for c in range(channels):
            grad_ref[q, c] = first[c : c + 1] * delta + second[c : c + 1] * delta_other


def mode_grad(modes, delta, count, channels):
    return pl.pallas_call(
        functools.partial(grad_kernel, count, channels),
        out_shape=jax.ShapeDtypeStruct((count, channels, channels, LANES), F32),
        compiler_params=params(6),
        name="mode_grad",
    )(modes, delta)


def per_device(devices, inputs, target, spectral_weight, local_weight, bias_term):
    samples, channels, rows, width = inputs.shape
    assert samples == 1
    field, target = inputs[0], target[0]
    height = rows * devices
    count = spectral_weight.shape[0]
    device = lax.axis_index("space")
    far = devices // 4

    place = np.arange(KY) // count
    offset = place // (2 * far) + 2 * (place // far % 2) + 4 * (place % far)
    order = (device ^ jnp.asarray(offset, jnp.int32)) * count + jnp.asarray(np.arange(KY) % count, jnp.int32)
    source = jnp.concatenate([order, order + KY])
    pick = (jnp.arange(LANES, dtype=jnp.int32)[:, None] == source[None, :]).astype(BF16)
    basis_table = row_basis_table(height, width)
    basis_t = dot(jnp.asarray(basis_table.T.copy()), pick).astype(BF16)
    tables = lax.dynamic_slice_in_dim(jnp.asarray(column_tables(height)), device * rows, rows, 0)
    mode_index = device * count + jnp.arange(count, dtype=jnp.int32)
    gain = jnp.broadcast_to(jnp.where(mode_index == 0, 1.0, 2.0).astype(F32)[:, None], (count, LANES))

    def exchange(value, mask):
        return lax.ppermute(value, "space", [(i, i ^ mask) for i in range(devices)])

    barrier = lax.optimization_barrier

    def beside(sent, received, work, state):
        if work is None:
            return received, state
        sent, state = barrier((sent, state))
        return barrier((received, work(state)))

    def reduce_modes(send, keep, work, state):
        received = exchange(send, 1).astype(F32)
        half = keep.shape[0] // 2
        send = (keep[half:] + received[half:]).astype(BF16)
        keep = keep[:half] + received[:half]
        received, state = beside(send, exchange(send, 2), work[0], state)
        total = keep + received.astype(F32)
        size = total.shape[0] // far
        pieces = [total[i * size : (i + 1) * size].astype(BF16) for i in range(1, far)]
        received, state = beside(pieces, [exchange(p, 4 * (i + 1)) for i, p in enumerate(pieces)], work[1], state)
        return [total[:size]] + received, state

    def gather_modes(own, extra, work, state):
        received, state = beside(own, [exchange(own, 4 * i) for i in range(1, far)], work[0], state)
        part = join([own] + received, extra)
        received, state = beside(part, exchange(part, 2), work[1], state)
        part = join([part, received], extra)
        return part, exchange(part, 1), state

    send, keep = analyse(field, basis_t, tables)
    bias = bias_term[:, None]
    splits = 4 if rows % 64 == 0 else 1
    step = rows // splits

    def local_work(i):
        if i >= splits:
            return None
        return lambda state: mix_local(field, forward_weight, bias, state, i * step, step)

    forward_weight = local_weight.T
    parts, state = reduce_modes(send, keep, [local_work(0), local_work(1)], None)
    mixed, modes = mix_modes(parts, spectral_weight, gain)
    first, second, local = gather_modes(mixed, 0, [local_work(2), local_work(3)], state)
    basis = lax.dot_general(pick, jnp.asarray(basis_table), (((0,), (0,)), ((), ())), preferred_element_type=F32)
    basis = basis.astype(BF16)
    delta, send, keep, sums = make_delta(local, target, first, second, basis, basis_t, tables)

    middle = rows // 2 if rows % 128 == 0 else rows

    def weight_work(first, end):
        if first == end:
            return None

        def work(state):
            out, grads = state
            out, grad = weight_grad(field, out, first, end - first)
            return out, grads + [grad]

        return work

    parts, (delta, grads) = reduce_modes(send, keep, [weight_work(0, middle), weight_work(middle, rows)], (delta, []))
    factor = math.sqrt(height * width)
    first_lane = pick[:1].astype(F32)
    back, delta_modes = mix_back(parts, grads, sums, first_lane, spectral_weight, gain, factor)
    extra = 3 * channels
    early = rows * 3 // 8 if rows % 128 == 0 else rows

    def back_work(first, end):
        return lambda state: (mix_back_local(local_weight, state[0], first, end - first),) + state[1:]

    def early_work(state):
        state = back_work(0, early)(state)
        return state[0], mode_grad(*state[1:], count, channels)

    first, second, (back_local, grad_spectral) = gather_modes(
        back, extra, [early_work, back_work(early, rows) if early < rows else None], (delta, modes, delta_modes)
    )
    grad_input = synthesise(back_local, first, second, basis, tables)
    grad_input, first, second = barrier((grad_input, first, second))
    shared = join_value(first[-extra:]) + join_value(second[-extra:])
    shared = shared / (samples * height * width)
    return (grad_input[None], grad_spectral, shared[:, :channels], shared[:, channels])


def solution(mesh):
    return jax.shard_map(
        functools.partial(per_device, mesh.shape["space"]),
        mesh=mesh,
        in_specs=(
            P("dom", None, "space", None),
            P("dom", None, "space", None),
            P("space", None, None, None),
            P(),
            P(),
        ),
        out_specs=(
            P("dom", None, "space", None),
            P("space", "dom", None, None),
            P("dom", None),
            P("dom"),
        ),
        check_vma=False,
    )
```

```python
import functools
import math

import jax
import jax.numpy as jnp
import ml_dtypes
import numpy as np
from jax import lax
from jax.experimental import pallas as pl
from jax.experimental.pallas import tpu as pltpu
from jax.sharding import PartitionSpec as P

KX = 64
KY = 64
LANES = 2 * KX
GROUP = 8
F32 = jnp.float32
BF16 = jnp.bfloat16
SCALE = math.sqrt(0.5)

dot = functools.partial(jnp.dot, preferred_element_type=F32)


def dot_last(a, b):
    return lax.dot_general(a, b, (((1,), (1,)), ((), ())), preferred_element_type=F32)


def params(mib):
    return pltpu.CompilerParams(vmem_limit_bytes=mib * 2**20)


def row_basis_table(height, width):
    angles = 2.0 * np.pi / width * (np.arange(KY)[:, None] * np.arange(width)[None, :] % width)
    factor = 1.0 / math.sqrt(height * width)
    table = np.concatenate([np.cos(angles) * factor, -np.sin(angles) * factor])
    return table.astype(np.float32).astype(ml_dtypes.bfloat16)


def column_tables(height):
    index = np.arange(KX)
    frequency = np.where(index < KX // 2, index, index + height - KX)
    angles = 2.0 * np.pi / height * (np.arange(height)[:, None] * frequency[None, :] % height)
    cosines, sines = np.cos(angles), np.sin(angles)

    def parts(table):
        high = table.astype(np.float32).astype(ml_dtypes.bfloat16)
        low = (table - high.astype(np.float64)).astype(np.float32).astype(ml_dtypes.bfloat16)
        return high, low

    synthesis = parts(np.concatenate([cosines, sines], axis=1))
    analysis = parts(np.concatenate([cosines, -sines, sines, cosines], axis=1))
    return np.concatenate(synthesis + analysis, axis=1)


def swap_halves(value):
    return pltpu.roll(value, LANES // 2, 1)


def real_lanes(shape):
    return lax.broadcasted_iota(jnp.int32, shape, 1) < LANES // 2


def column_analysis(row_modes, tables_ref):
    rows = row_modes[0].shape[0]
    first, second = LANES * 2, LANES * 3
    high = [tables_ref[:, first : first + LANES], tables_ref[:, second : second + LANES]]
    low = [tables_ref[:, first + 2 * LANES : first + 3 * LANES], tables_ref[:, second + 2 * LANES : second + 3 * LANES]]
    flipped = [value.T for value in row_modes]
    parts = [[value[:KY] for value in flipped], [value[KY:] for value in flipped]]
    parts = [jnp.concatenate(part, axis=0) for part in parts]
    if rows % 128 == 0:
        parts = [jnp.concatenate(parts, axis=1)]
        high = [jnp.concatenate(high, axis=0)]
        low = [jnp.concatenate(low, axis=0)]
    total = 0.0
    for part, table_high, table_low in zip(parts, high, low):
        part_high = part.astype(BF16)
        part_low = (part - part_high.astype(F32)).astype(BF16)
        total += dot(part_high, table_high) + dot(part_low, table_high) + dot(part_high, table_low)
    return [total[i * KY : (i + 1) * KY] for i in range(len(row_modes))]


def column_synthesis(modes_ref, channel, channels, tables_ref):
    modes = modes_ref[pl.ds(channel, KY, stride=channels), :]
    real = real_lanes(modes.shape)
    both = jnp.concatenate([jnp.where(real, modes, -modes), swap_halves(modes)], axis=0).astype(BF16)
    both = jnp.concatenate([both, both], axis=1)
    return dot_last(tables_ref[:, : 2 * LANES], both).astype(BF16)


def twice_delta(value, target):
    cdf = 1.0 + lax.erf(value)
    density = jnp.exp2(value * (value * -math.log2(math.e))) * (2.0 / math.sqrt(math.pi))
    value, cdf, density = value.astype(BF16), cdf.astype(BF16), density.astype(BF16)
    return (value * cdf * BF16(SCALE) - target) * (cdf + value * density)


def store_modes(product, first, block, tables_ref, modes):
    rows = product.shape[0] // block
    channels = modes.shape[0] // KY
    parts = column_analysis([product[i * rows : (i + 1) * rows] for i in range(block)], tables_ref)
    for i, part in enumerate(parts):
        modes[pl.ds(first + i, KY, stride=channels), :] = part


def emit_halves(modes, send_ref, keep_ref):
    half = modes.shape[0] // 2
    keep_ref[...] = modes[:half]
    send_ref[...] = modes[half:].astype(BF16)


VMEM = pl.BlockSpec(memory_space=pltpu.VMEM)
HBM = pl.BlockSpec(memory_space=pl.ANY)


def in_vmem(array):
    return pltpu.with_memory_space_constraint(array, pltpu.VMEM)


def in_hbm(array):
    return pltpu.with_memory_space_constraint(array, pltpu.HBM)


def half_shapes(channels):
    half = KY // 2 * channels
    return [jax.ShapeDtypeStruct((half, LANES), BF16), jax.ShapeDtypeStruct((half, LANES), F32)]


def analysis_kernel(block, field_ref, basis_ref, tables_ref, send_ref, keep_ref, held_ref, modes, sems):
    channels, rows, width = field_ref.shape
    copies = [pltpu.make_async_copy(field_ref.at[i], held_ref.at[i], sems.at[i]) for i in range(channels)]
    for copy in copies:
        copy.start()
    product = None
    for start in range(0, channels + block, block):
        before, product = product, None
        if start < channels:
            for copy in copies[start : start + block]:
                copy.wait()
            product = dot(held_ref[pl.ds(start, block)].reshape(block * rows, width), basis_ref[...])
        if before is not None:
            store_modes(before, start - block, block, tables_ref, modes)
    emit_halves(modes, send_ref, keep_ref)


def analyse(field, basis_t, tables, block=2):
    channels = field.shape[0]
    return pl.pallas_call(
        functools.partial(analysis_kernel, block),
        in_specs=[HBM, VMEM, VMEM],
        out_specs=[VMEM] * 2,
        out_shape=half_shapes(channels),
        scratch_shapes=[pltpu.VMEM(field.shape, BF16), pltpu.VMEM((KY * channels, LANES), F32), pltpu.SemaphoreType.DMA((channels,))],
        compiler_params=params(24),
        name="analyse",
    )(in_hbm(field), basis_t, tables)


def group_rows(value, start):
    channels, _, width = value.shape
    return value[:, start : start + GROUP, :].reshape(channels * GROUP, width).astype(BF16)


def picks(channels):
    size = channels * GROUP
    wide = lax.broadcasted_iota(jnp.int32, (channels, size), 1) // GROUP
    return (wide == lax.broadcasted_iota(jnp.int32, (channels, size), 0)).astype(BF16)


def same_row(size):
    row = lax.broadcasted_iota(jnp.int32, (size, size), 0) % GROUP
    return row == lax.broadcasted_iota(jnp.int32, (size, size), 1) % GROUP


def spread_weight(weight):
    pick = picks(weight.shape[0])
    wide = dot(weight, pick).astype(BF16)
    full = lax.dot_general(pick, wide, (((0,), (0,)), ((), ())), preferred_element_type=F32)
    return jnp.where(same_row(pick.shape[1]), full, 0.0).astype(BF16)


def fetch_rows(field_ref, held, sems, first, block):
    copies = [
        pltpu.make_async_copy(field_ref.at[:, pl.ds(first + i * block, block)], held.at[i], sems.at[i])
        for i in range(held.shape[0])
    ]
    for copy in copies:
        copy.start()
    return copies


def local_kernel(first, chunk, field_ref, weight_ref, bias_ref, *rest):
    out_ref, held, sems = rest[-3:]
    blocks, channels, block, width = held.shape
    copies = fetch_rows(field_ref, held, sems, first, block)
    weight = spread_weight(weight_ref[...])
    bias = lax.dot_general(
        picks(channels).astype(F32), bias_ref[...], (((0,), (0,)), ((), ())),
        precision=lax.Precision.HIGHEST, preferred_element_type=F32,
    )
    for i, copy in enumerate(copies):
        copy.wait()
        rows = slice(first + i * block, first + (i + 1) * block)
        for start in range(0, width, chunk):
            columns = pl.ds(start, chunk)
            field = held[i, :, :, columns].astype(F32)
            parts = []
            for group in range(0, block, GROUP):
                part = (dot(weight, group_rows(field, group)) + bias) * SCALE
                parts.append(part.reshape(channels, GROUP, chunk))
            out_ref[:, rows, columns] = jnp.concatenate(parts, axis=1).astype(BF16)


def mix_local(field, weight, bias, out, first, count, block=16, chunk=512):
    more = [] if out is None else [in_vmem(out)]
    return pl.pallas_call(
        functools.partial(local_kernel, first, chunk),
        in_specs=[HBM] + [VMEM] * (2 + len(more)),
        out_specs=VMEM,
        out_shape=pltpu.VMEM(field.shape, BF16),
        scratch_shapes=row_scratch(field, count, block, count // block),
        input_output_aliases={3: 0} if more else {},
        compiler_params=params(8),
        name="mix_local",
    )(in_hbm(field), weight, bias, *more)


def row_copies(field_ref, held, sems, first, count):
    slots, _, block, _ = held.shape
    return [
        pltpu.make_async_copy(
            field_ref.at[:, pl.ds(first + i * block, block)], held.at[i % slots], sems.at[i % slots]
        )
        for i in range(count // block)
    ]


def row_scratch(field, count, block, slots):
    channels, _, width = field.shape
    slots = min(slots, count // block)
    return [pltpu.VMEM((slots, channels, block, width), BF16), pltpu.SemaphoreType.DMA((slots,))]


def weight_kernel(first, count, chunk, field_ref, delta_ref, _, grad_ref, held, sems):
    width = field_ref.shape[2]
    slots, _, block, _ = held.shape
    copies = row_copies(field_ref, held, sems, first, count)
    for copy in copies[:slots]:
        copy.start()
    grad = jnp.zeros(grad_ref.shape, F32)
    for i, copy in enumerate(copies):
        copy.wait()
        here = slice(first + i * block, first + (i + 1) * block)
        for start in range(0, width, chunk):
            columns = pl.ds(start, chunk)
            field = held[i % slots, :, :, columns].astype(F32)
            delta = delta_ref[:, here, columns].astype(F32)
            for group in range(0, block, GROUP):
                grad += dot_last(group_rows(field, group), group_rows(delta, group))
        if i + slots < len(copies):
            copies[i + slots].start()
    grad_ref[...] = grad * 0.5


def weight_grad(field, delta, first, count, block=16, chunk=1024):
    channels = field.shape[0]
    return pl.pallas_call(
        functools.partial(weight_kernel, first, count, chunk),
        in_specs=[HBM, VMEM],
        out_specs=[VMEM] * 2,
        out_shape=[pltpu.VMEM(delta.shape, BF16), jax.ShapeDtypeStruct((channels * GROUP,) * 2, F32)],
        input_output_aliases={1: 0},
        scratch_shapes=row_scratch(field, count, block, 3),
        compiler_params=params(10),
        name="weight_grad",
    )(in_hbm(field), in_vmem(delta))


def back_kernel(first, count, block, chunk, weight_ref, delta_ref, out_ref):
    channels, _, width = delta_ref.shape
    weight = spread_weight(weight_ref[...]) * 0.5
    for row in range(first, first + count, block):
        here = slice(row, row + block)
        for start in range(0, width, chunk):
            columns = pl.ds(start, chunk)
            delta = delta_ref[:, here, columns].astype(F32)
            parts = []
            for group in range(0, block, GROUP):
                parts.append(dot(weight, group_rows(delta, group)).reshape(channels, GROUP, chunk))
            out_ref[:, here, columns] = jnp.concatenate(parts, axis=1).astype(BF16)


def mix_back_local(weight, delta, first, count, block=16, chunk=512):
    return pl.pallas_call(
        functools.partial(back_kernel, first, count, block, chunk),
        in_specs=[VMEM, VMEM],
        out_specs=VMEM,
        out_shape=pltpu.VMEM(delta.shape, BF16),
        input_output_aliases={1: 0},
        compiler_params=params(8),
        name="mix_back_local",
    )(weight, in_vmem(delta))


def load_modes(modes, first_ref, second_ref, scale=1.0):
    half = modes.shape[0] // 2
    modes[:half] = first_ref[:half].astype(F32) * scale
    modes[half:] = second_ref[:half].astype(F32) * scale


def delta_kernel(
    block, chunk, local_ref, target_ref, first_ref, second_ref, basis_ref, basis_t_ref, tables_ref,
    delta_ref, send_ref, keep_ref, sums_ref, mixed, modes, held, sems,
):
    channels, rows, width = local_ref.shape
    steps = channels // block
    slots = held.shape[0]
    copies = [
        pltpu.make_async_copy(target_ref.at[pl.ds(i * block, block)], held.at[i % slots], sems.at[i % slots])
        for i in range(steps)
    ]
    for copy in copies[: slots - 1]:
        copy.start()
    load_modes(mixed, first_ref, second_ref, SCALE)

    def spectra_of(step):
        first = step * block
        return jnp.concatenate([column_synthesis(mixed, first + i, channels, tables_ref) for i in range(block)], axis=0)

    def finish(product, step):
        store_modes(product, step * block, block, tables_ref, modes)
        sums = jnp.sum(product.reshape(block, rows, LANES), axis=1)
        sums_ref[pl.ds(step * block, block), :] = sums

    product = None
    spectra = spectra_of(0)
    for step in range(steps):
        if step + slots - 1 < steps:
            copies[step + slots - 1].start()
        copies[step].wait()
        here, slot = pl.ds(step * block, block), step % slots
        before, product = product, jnp.zeros((block * rows, LANES), F32)
        for start in range(0, width, chunk):
            columns = pl.ds(start, chunk)
            local = local_ref[here, :, columns].reshape(block * rows, chunk).astype(F32)
            target = held[slot, :, :, columns].reshape(block * rows, chunk)
            delta = twice_delta(dot(spectra, basis_ref[:, columns]) + local, target)
            delta_ref[here, :, columns] = delta.reshape(block, rows, chunk)
            product += dot(delta, basis_t_ref[columns, :])
        product *= 0.5
        if before is not None:
            finish(before, step - 1)
        if step + 1 < steps:
            spectra = spectra_of(step + 1)
    finish(product, steps - 1)
    emit_halves(modes, send_ref, keep_ref)


def make_delta(local, target, first, second, basis, basis_t, tables, block=4, chunk=2048, slots=3):
    channels, rows, width = local.shape
    scratch = pltpu.VMEM((KY * channels, LANES), F32)
    return pl.pallas_call(
        functools.partial(delta_kernel, block, chunk),
        in_specs=[VMEM, HBM] + [VMEM] * 5,
        out_specs=[VMEM] * 4,
        out_shape=[pltpu.VMEM(local.shape, BF16)]
        + half_shapes(channels)
        + [jax.ShapeDtypeStruct((channels, LANES), F32)],
        scratch_shapes=[
            scratch, scratch, pltpu.VMEM((slots, block, rows, width), BF16), pltpu.SemaphoreType.DMA((slots,))
        ],
        input_output_aliases={0: 0},
        compiler_params=params(18),
        name="make_delta",
    )(in_vmem(local), in_hbm(target), first, second, basis, basis_t, tables)


def synthesis_kernel(
    block, chunk, local_ref, first_ref, second_ref, basis_ref, tables_ref, sum_ref, out_ref, modes, sems
):
    channels, rows, width = local_ref.shape
    steps = channels // block
    load_modes(modes, first_ref, second_ref)

    def spectra_of(step):
        first = step * block
        return jnp.concatenate([column_synthesis(modes, first + i, channels, tables_ref) for i in range(block)], axis=0)

    copies = []
    spectra = spectra_of(0)
    for step in range(steps):
        here = pl.ds(step * block, block)
        for start in range(0, width, chunk):
            columns = pl.ds(start, chunk)
            local = local_ref[here, :, columns].reshape(block * rows, chunk).astype(F32)
            value = dot(spectra, basis_ref[:, columns]) + local
            sum_ref[here, :, columns] = value.astype(BF16).reshape(block, rows, chunk)
        copies.append(pltpu.make_async_copy(sum_ref.at[here], out_ref.at[here], sems.at[step]))
        copies[step].start()
        if step + 1 < steps:
            spectra = spectra_of(step + 1)
    for copy in copies:
        copy.wait()


def synthesise(local, first, second, basis, tables, block=4, chunk=2048):
    channels = local.shape[0]
    return pl.pallas_call(
        functools.partial(synthesis_kernel, block, chunk),
        in_specs=[VMEM] * 5,
        out_specs=[VMEM, HBM],
        out_shape=[pltpu.VMEM(local.shape, BF16), jax.ShapeDtypeStruct(local.shape, BF16)],
        scratch_shapes=[pltpu.VMEM((KY * channels, LANES), F32), pltpu.SemaphoreType.DMA((channels // block,))],
        input_output_aliases={0: 0},
        compiler_params=params(8),
        name="synthesise",
    )(in_vmem(local), first, second, basis, tables)[1]


def sum_parts(refs):
    return functools.reduce(lambda a, b: a + b, [ref[...].astype(F32) for ref in refs])


def mix_modes_kernel(count, channels, *refs):
    parts, (weight_ref, gain_ref, mixed_ref, modes_ref) = refs[:-4], refs[-4:]
    modes_ref[...] = sum_parts(parts)
    real = real_lanes((channels, LANES))
    for q in range(count):
        rows = slice(q * channels, (q + 1) * channels)
        modes = modes_ref[rows]
        other = swap_halves(modes)
        first, second = jnp.where(real, modes, other), jnp.where(real, other, -modes)
        direct = jnp.zeros((channels, LANES), F32)
        crossed = jnp.zeros((channels, LANES), F32)
        for c in range(channels):
            weight = weight_ref[q, c]
            direct += first[c : c + 1] * weight
            crossed += second[c : c + 1] * weight
        mixed_ref[rows] = ((direct + swap_halves(crossed)) * gain_ref[q : q + 1]).astype(BF16)


def mix_modes(parts, weight, gain):
    count, channels = weight.shape[:2]
    return pl.pallas_call(
        functools.partial(mix_modes_kernel, count, channels),
        out_shape=[
            jax.ShapeDtypeStruct((count * channels, LANES), BF16),
            jax.ShapeDtypeStruct((count * channels, LANES), F32),
        ],
        compiler_params=params(3),
        name="mix_modes",
    )(*parts, weight, gain)


def split_value(value):
    parts = []
    for _ in range(3):
        part = value.astype(BF16)
        value = value - part.astype(F32)
        parts.append(part)
    return jnp.concatenate(parts, axis=0)


def join_value(parts):
    size = parts.shape[0] // 3
    parts = parts.astype(F32)
    return (parts[:size] + parts[size : 2 * size]) + parts[2 * size :]


def tree(values):
    while len(values) > 1:
        values = [values[i] + values[i + 1] for i in range(0, len(values), 2)]
    return values[0]


def shared_terms(total, sums, first_lane, factor):
    channels, size = sums.shape[0], total.shape[0]
    total = jnp.where(same_row(size), total, 0.0)
    total = jnp.sum(total.reshape(channels, GROUP, size), axis=1)
    wide = lax.broadcasted_iota(jnp.int32, (LANES, size), 1) // GROUP
    pick = (wide == lax.broadcasted_iota(jnp.int32, (LANES, size), 0)).astype(F32)
    weight = lax.dot_general(
        total, pick, (((1,), (1,)), ((), ())), precision=lax.Precision.HIGHEST, preferred_element_type=F32
    )
    bias = jnp.sum(sums * first_lane, axis=1, keepdims=True) * factor
    lane = lax.broadcasted_iota(jnp.int32, weight.shape, 1)
    return jnp.where(lane == channels, bias, weight)


def mix_back_kernel(count, channels, factor, terms, *refs):
    parts, grads, (sums_ref, lane_ref, weight_ref, gain_ref, back_ref, delta_ref) = (
        refs[: -6 - terms], refs[-6 - terms : -6], refs[-6:]
    )
    delta_ref[...] = sum_parts(parts)
    real = real_lanes((channels, LANES))
    for q in range(count):
        rows = slice(q * channels, (q + 1) * channels)
        delta = delta_ref[rows] * gain_ref[q : q + 1]
        delta_ref[rows] = delta
        other = swap_halves(delta)
        first, second = jnp.where(real, delta, -other), jnp.where(real, other, delta)
        direct, crossed = [], []
        for c in range(channels):
            weight = weight_ref[q, c]
            direct.append(jnp.sum(first * weight, axis=0, keepdims=True))
            crossed.append(jnp.sum(second * weight, axis=0, keepdims=True))
        direct, crossed = jnp.concatenate(direct, axis=0), jnp.concatenate(crossed, axis=0)
        back_ref[rows] = (direct + swap_halves(crossed)).astype(BF16)
    shared = shared_terms(sum_parts(grads), sums_ref[...], lane_ref[...], factor)
    back_ref[count * channels :] = split_value(shared)


def mix_back(parts, grads, sums, first_lane, weight, gain, factor):
    count, channels = weight.shape[:2]
    return pl.pallas_call(
        functools.partial(mix_back_kernel, count, channels, factor, len(grads)),
        out_shape=[
            jax.ShapeDtypeStruct(((count + 3) * channels, LANES), BF16),
            jax.ShapeDtypeStruct((count * channels, LANES), F32),
        ],
        compiler_params=params(6),
        name="mix_back",
    )(*parts, *grads, sums, first_lane, weight, gain)


def join_kernel(extra, *refs):
    parts, out_ref = refs[:-1], refs[-1]
    size = parts[0].shape[0] - extra
    for i, part in enumerate(parts):
        out_ref[i * size : (i + 1) * size] = part[:size]
    if extra:
        out_ref[len(parts) * size :] = split_value(tree([join_value(part[size:]) for part in parts]))


def join(parts, extra):
    rows = (parts[0].shape[0] - extra) * len(parts) + extra
    return pl.pallas_call(
        functools.partial(join_kernel, extra),
        out_shape=jax.ShapeDtypeStruct((rows, LANES), BF16),
        compiler_params=params(4),
        name="join",
    )(*parts)


def grad_kernel(count, channels, modes_ref, delta_ref, grad_ref):
    real = real_lanes((channels, LANES))
    for q in range(count):
        rows = slice(q * channels, (q + 1) * channels)
        modes, delta = modes_ref[rows], delta_ref[rows]
        other, delta_other = swap_halves(modes), swap_halves(delta)
        first, second = jnp.where(real, modes, other), jnp.where(real, other, -modes)
        for c in range(channels):
            grad_ref[q, c] = first[c : c + 1] * delta + second[c : c + 1] * delta_other


def mode_grad(modes, delta, count, channels):
    return pl.pallas_call(
        functools.partial(grad_kernel, count, channels),
        out_shape=jax.ShapeDtypeStruct((count, channels, channels, LANES), F32),
        compiler_params=params(6),
        name="mode_grad",
    )(modes, delta)


def per_device(devices, inputs, target, spectral_weight, local_weight, bias_term):
    samples, channels, rows, width = inputs.shape
    assert samples == 1
    field, target = inputs[0], target[0]
    height = rows * devices
    count = spectral_weight.shape[0]
    device = lax.axis_index("space")
    far = devices // 4

    place = np.arange(KY) // count
    offset = place // (2 * far) + 2 * (place // far % 2) + 4 * (place % far)
    order = (device ^ jnp.asarray(offset, jnp.int32)) * count + jnp.asarray(np.arange(KY) % count, jnp.int32)
    source = jnp.concatenate([order, order + KY])
    pick = (jnp.arange(LANES, dtype=jnp.int32)[:, None] == source[None, :]).astype(BF16)
    basis_table = row_basis_table(height, width)
    basis_t = dot(jnp.asarray(basis_table.T.copy()), pick).astype(BF16)
    tables = lax.dynamic_slice_in_dim(jnp.asarray(column_tables(height)), device * rows, rows, 0)
    mode_index = device * count + jnp.arange(count, dtype=jnp.int32)
    gain = jnp.broadcast_to(jnp.where(mode_index == 0, 1.0, 2.0).astype(F32)[:, None], (count, LANES))

    def exchange(value, mask):
        return lax.ppermute(value, "space", [(i, i ^ mask) for i in range(devices)])

    barrier = lax.optimization_barrier

    def beside(sent, received, work, state):
        if work is None:
            return received, state
        sent, state = barrier((sent, state))
        return barrier((received, work(state)))

    def reduce_modes(send, keep, work, state):
        received = exchange(send, 1).astype(F32)
        half = keep.shape[0] // 2
        send = (keep[half:] + received[half:]).astype(BF16)
        keep = keep[:half] + received[:half]
        received, state = beside(send, exchange(send, 2), work[0], state)
        total = keep + received.astype(F32)
        size = total.shape[0] // far
        pieces = [total[i * size : (i + 1) * size].astype(BF16) for i in range(1, far)]
        received, state = beside(pieces, [exchange(p, 4 * (i + 1)) for i, p in enumerate(pieces)], work[1], state)
        return [total[:size]] + received, state

    def gather_modes(own, extra, work, state):
        received, state = beside(own, [exchange(own, 4 * i) for i in range(1, far)], work[0], state)
        part = join([own] + received, extra)
        received, state = beside(part, exchange(part, 2), work[1], state)
        part = join([part, received], extra)
        return part, exchange(part, 1), state

    send, keep = analyse(field, basis_t, tables)
    bias = bias_term[:, None]
    splits = 4 if rows % 64 == 0 else 1
    step = rows // splits

    def local_work(i):
        if i >= splits:
            return None
        return lambda state: mix_local(field, forward_weight, bias, state, i * step, step)

    forward_weight = local_weight.T
    parts, state = reduce_modes(send, keep, [local_work(0), local_work(1)], None)
    mixed, modes = mix_modes(parts, spectral_weight, gain)
    first, second, local = gather_modes(mixed, 0, [local_work(2), local_work(3)], state)
    basis = lax.dot_general(pick, jnp.asarray(basis_table), (((0,), (0,)), ((), ())), preferred_element_type=F32)
    basis = basis.astype(BF16)
    delta, send, keep, sums = make_delta(local, target, first, second, basis, basis_t, tables)

    middle = rows // 2 if rows % 128 == 0 else rows

    def weight_work(first, end):
        if first == end:
            return None

        def work(state):
            out, grads = state
            out, grad = weight_grad(field, out, first, end - first)
            return out, grads + [grad]

        return work

    parts, (delta, grads) = reduce_modes(send, keep, [weight_work(0, middle), weight_work(middle, rows)], (delta, []))
    factor = math.sqrt(height * width)
    first_lane = pick[:1].astype(F32)
    back, delta_modes = mix_back(parts, grads, sums, first_lane, spectral_weight, gain, factor)
    extra = 3 * channels
    early = rows * 3 // 8 if rows % 128 == 0 else rows

    def back_work(first, end):
        return lambda state: (mix_back_local(local_weight, state[0], first, end - first),) + state[1:]

    def early_work(state):
        state = back_work(0, early)(state)
        return state[0], mode_grad(*state[1:], count, channels)

    first, second, (back_local, grad_spectral) = gather_modes(
        back, extra, [early_work, back_work(early, rows) if early < rows else None], (delta, modes, delta_modes)
    )
    grad_input = synthesise(back_local, first, second, basis, tables)
    grad_input, first, second = barrier((grad_input, first, second))
    shared = join_value(first[-extra:]) + join_value(second[-extra:])
    shared = shared / (samples * height * width)
    return (grad_input[None], grad_spectral, shared[:, :channels], shared[:, channels])


def solution(mesh):
    return jax.shard_map(
        functools.partial(per_device, mesh.shape["space"]),
        mesh=mesh,
        in_specs=(
            P("dom", None, "space", None),
            P("dom", None, "space", None),
            P("space", None, None, None),
            P(),
            P(),
        ),
        out_specs=(
            P("dom", None, "space", None),
            P("space", "dom", None, None),
            P("dom", None),
            P("dom"),
        ),
        check_vma=False,
    )
```
